32 devices in a mesh: row: 4 (over y, x), col: 4 (over z), rep: 2 (over core).
Axes of the slice: x: 2, y: 2, z: 4, core: 2. Of those that a mesh axis runs over, the one named last changes fastest.
Arguments:
- queries: bfloat16 [2048, 4096], P(('rep', 'row'), 'col'), may hold values from -6 to 6
- key_vectors: bfloat16 [2048, 4096], P(('rep', 'row'), 'col'), may hold values from -6 to 6
- value_vectors: bfloat16 [2048, 4096], P(('rep', 'row'), 'col'), may hold values from -12 to 12
- cotangent: bfloat16 [2048, 6144], P(('rep', 'row'), 'col'), may hold values from -6 to 6
- out_weight: bfloat16 [4096, 6144], P('row', 'col'), may hold values from -0.09375 to 0.09375
Outputs:
- projected: bfloat16 [2048, 6144], P(('rep', 'row'), 'col')
- grad_query: bfloat16 [2048, 4096], P(('rep', 'row'), 'col')
- grad_key: bfloat16 [2048, 4096], P(('rep', 'row'), 'col')
- grad_value: bfloat16 [2048, 4096], P(('rep', 'row'), 'col')
- grad_weight: bfloat16 [4096, 6144], P('row', 'col')
The draws below stay inside these ranges and needn't reach their ends.
All inputs are finite; a program needn't handle non-finite values.
Results may differ from the reference program's by a relative error of at most 0.011.
Values may be sent and summed in bfloat16 or wider, within the bound.
No kernel may reach another device: no remote copies, remote signals or barrier semaphores. Data moves between devices by JAX's collectives and lax.ppermute only.
A program may use at most 128 MiB of HBM per device.

```python
import jax
import jax.numpy as jnp
from jax import lax

D = 6144
HSZ = 128
PATCH = 256
HEADS = 32
HD = 4096
TOKENS = 2048


def draw_queries(key, part):
    key = jax.random.fold_in(key, 1)
    return jnp.clip(1.5 * jax.random.normal(key, (TOKENS, HD), jnp.float32), -6.0, 6.0).astype(jnp.bfloat16)


def draw_key_vectors(key, part):
    key = jax.random.fold_in(key, 2)
    return jnp.clip(1.5 * jax.random.normal(key, (TOKENS, HD), jnp.float32), -6.0, 6.0).astype(jnp.bfloat16)


def levels(own_key, dims, split, low, top_value):
    factor_of, own = 1.0, jax.random.fold_in(own_key, 6)
    for axis_at, shards_of in split:
        heights = jnp.exp(jax.random.uniform(jax.random.fold_in(own, axis_at), (shards_of,), jnp.float32, low / len(split), top_value / len(split)))
        factor_of = factor_of * jnp.repeat(heights, dims[axis_at] // shards_of).reshape([-1 if axis == axis_at else 1 for axis in range(len(dims))])
    return factor_of


def noise(stream_key, shape, deviation, limit, pieces=(), kind=jnp.bfloat16):
    entries = deviation * jax.random.normal(stream_key, shape, jnp.float32)
    if pieces:
        entries = entries * levels(stream_key, shape, pieces, -0.22, 0.18)
    return jnp.clip(entries, -limit, limit).astype(kind)


def setup_inputs(seed: int = 0) -> dict:
    streams_of = jax.random.split(jax.random.key(seed), 6)
    return {
        "queries": draw_queries(jax.random.fold_in(streams_of[5], 71), 0),
        "key_vectors": draw_key_vectors(jax.random.fold_in(streams_of[5], 71), 0),
        "value_vectors": noise(streams_of[2], (TOKENS, HD), 2.0, 12.0, ((0, 8), (1, 4))),
        "cotangent": noise(streams_of[3], (TOKENS, D), 1.0, 6.0, ((0, 8), (1, 4))),
        "out_weight": noise(streams_of[4], (HD, D), HD ** -0.5, 0.09375, ((0, 4), (1, 4))),
    }


def softmax_weights(query_blk, key_blk):
    scores = jnp.einsum("bqhd,bkhd->bhqk", query_blk.astype(jnp.float32), key_blk.astype(jnp.float32), precision=lax.Precision.HIGHEST) * HSZ ** -0.5
    peak = jnp.max(scores, axis=-1, keepdims=True)
    lifted = jnp.exp(scores - peak)
    return lifted / jnp.sum(lifted, axis=-1, keepdims=True)


def forward_image(blocks):
    query_blk, key_blk, value_blk = [member[None] for member in blocks]
    prob_low = lax.optimization_barrier(softmax_weights(query_blk, key_blk).astype(jnp.bfloat16))
    head_out = jnp.einsum("bhqk,bkhd->bqhd", prob_low.astype(jnp.float32), value_blk.astype(jnp.float32), precision=lax.Precision.HIGHEST)
    return head_out.astype(jnp.bfloat16)[0]


def backward_image(blocks):
    query_blk, key_blk, value_blk, grad_blk = [member[None] for member in blocks]
    prob_full = softmax_weights(query_blk, key_blk)
    prob_low = lax.optimization_barrier(prob_full.astype(jnp.bfloat16))
    grad_prob = jnp.einsum("bqhd,bkhd->bhqk", grad_blk.astype(jnp.float32), value_blk.astype(jnp.float32), precision=lax.Precision.HIGHEST)
    row_delta = jnp.sum(prob_full * grad_prob, axis=-1, keepdims=True)
    grad_score = lax.optimization_barrier((prob_full * (grad_prob - row_delta) * HSZ ** -0.5).astype(jnp.bfloat16))
    score_wide = grad_score.astype(jnp.float32)
    grad_query = jnp.einsum("bhqk,bkhd->bqhd", score_wide, key_blk.astype(jnp.float32), precision=lax.Precision.HIGHEST)
    grad_key = jnp.einsum("bhqk,bqhd->bkhd", score_wide, query_blk.astype(jnp.float32), precision=lax.Precision.HIGHEST)
    grad_value = jnp.einsum("bhqk,bqhd->bkhd", prob_low.astype(jnp.float32), grad_blk.astype(jnp.float32), precision=lax.Precision.HIGHEST)
    return (grad_query.astype(jnp.bfloat16)[0], grad_key.astype(jnp.bfloat16)[0], grad_value.astype(jnp.bfloat16)[0])


def reference(queries, key_vectors, value_vectors, cotangent, out_weight):
    images = TOKENS // PATCH
    shaped = (images, PATCH, HEADS, HSZ)
    query_all = queries.reshape(shaped)
    key_all = key_vectors.reshape(shaped)
    value_all = value_vectors.reshape(shaped)
    head_out = lax.map(forward_image, (query_all, key_all, value_all)).reshape(TOKENS, HD)
    projected = jnp.dot(head_out, out_weight, preferred_element_type=jnp.float32).astype(jnp.bfloat16)
    grad_heads = jnp.dot(cotangent, out_weight.T, preferred_element_type=jnp.float32).astype(jnp.bfloat16)
    grad_query, grad_key, grad_value = lax.map(backward_image, (query_all, key_all, value_all, grad_heads.reshape(shaped)))
    weight_sum = lax.dot_general(head_out, cotangent, (((0,), (0,)), ((), ())), preferred_element_type=jnp.float32)
    grad_weight = (weight_sum * TOKENS ** -0.5).astype(jnp.bfloat16)
    return (projected, grad_query.reshape(TOKENS, HD), grad_key.reshape(TOKENS, HD), grad_value.reshape(TOKENS, HD), grad_weight)
```

```python
import functools

import jax
import jax.numpy as jnp
from jax import lax
from jax.experimental import pallas as pl
from jax.experimental.pallas import tpu as pltpu
from jax.sharding import PartitionSpec as P

HSZ = 128
PATCH = 256
SCALE = HSZ ** (-0.5)

NT = (((1,), (1,)), ((), ()))
TN = (((0,), (0,)), ((), ()))


def dot(a, b, dims=(((1,), (0,)), ((), ()))):
    return lax.dot_general(a, b, dims, preferred_element_type=jnp.float32)


def softmax_block(q, k):
    scores = dot(q, k, NT) * SCALE
    lifted = jnp.exp(scores - jnp.max(scores, axis=-1, keepdims=True))
    return lifted / jnp.sum(lifted, axis=-1, keepdims=True)


def forward_kernel(q_ref, k_ref, v_ref, o_ref):
    for lo in range(0, q_ref.shape[1], HSZ):
        cols = slice(lo, lo + HSZ)
        prob = softmax_block(q_ref[:, cols], k_ref[:, cols]).astype(jnp.bfloat16)
        o_ref[:, cols] = dot(prob, v_ref[:, cols]).astype(jnp.bfloat16)


def backward_kernel(q_ref, k_ref, v_ref, g_ref, *refs):
    gq_ref, gk_ref, gv_ref = refs[-3:]
    for lo in range(0, q_ref.shape[1], HSZ):
        cols = slice(lo, lo + HSZ)
        q, k, v, g = q_ref[:, cols], k_ref[:, cols], v_ref[:, cols], g_ref[:, cols]
        prob = softmax_block(q, k)
        grad_prob = dot(g, v, NT)
        delta = jnp.sum(prob * grad_prob, axis=-1, keepdims=True)
        grad_score = (prob * (grad_prob - delta) * SCALE).astype(jnp.bfloat16)
        gq_ref[:, cols] = dot(grad_score, k).astype(jnp.bfloat16)
        gk_ref[:, cols] = dot(grad_score, q, TN).astype(jnp.bfloat16)
        gv_ref[:, cols] = dot(prob.astype(jnp.bfloat16), g, TN).astype(jnp.bfloat16)


def heads_per_step(width):
    return 2 if width % (2 * HSZ) == 0 else 1


def attention(q, k, v, at, width):
    wide = heads_per_step(width) * HSZ
    spec = pl.BlockSpec((PATCH, wide), lambda i, h: (i, h + at // wide))
    macs = 2 * q.shape[0] * PATCH * width
    return pl.pallas_call(
        forward_kernel,
        grid=(q.shape[0] // PATCH, width // wide),
        in_specs=[spec] * 3,
        out_specs=pl.BlockSpec((PATCH, wide), lambda i, h: (i, h)),
        out_shape=jax.ShapeDtypeStruct((q.shape[0], width), jnp.bfloat16),
        cost_estimate=pl.CostEstimate(
            flops=2 * macs, bytes_accessed=8 * q.shape[0] * width, transcendentals=macs // HSZ // 2
        ),
    )(q, k, v)


def attention_grads(q, k, v, g, at, before):
    width = g.shape[1]
    wide = heads_per_step(width) * HSZ
    spec = pl.BlockSpec((PATCH, wide), lambda i, h: (i, h + at // wide))
    macs = 5 * q.shape[0] * PATCH * width
    return pl.pallas_call(
        backward_kernel,
        grid=(q.shape[0] // PATCH, width // wide),
        in_specs=[spec] * 3
        + [pl.BlockSpec((PATCH, wide), lambda i, h: (i, h))]
        + [pl.BlockSpec(memory_space=pl.ANY)] * len(before),
        out_specs=[spec] * 3,
        out_shape=[jax.ShapeDtypeStruct(q.shape, jnp.bfloat16)] * 3,
        input_output_aliases={4 + i: i for i in range(len(before))},
        cost_estimate=pl.CostEstimate(
            flops=2 * macs, bytes_accessed=14 * q.shape[0] * width, transcendentals=macs // HSZ // 5
        ),
    )(q, k, v, g, *before)


def flip(x, axis, bit):
    return lax.ppermute(x, axis, [(i, i ^ bit) for i in range(lax.axis_size(axis))])


def xor_pick(blocks, m):
    odd, high = (m & 1) == 1, (m & 2) == 2
    a, b, c, d = blocks
    a, b, c, d = (
        jnp.where(odd, b, a),
        jnp.where(odd, a, b),
        jnp.where(odd, d, c),
        jnp.where(odd, c, d),
    )
    return [
        jnp.where(high, c, a),
        jnp.where(high, d, b),
        jnp.where(high, a, c),
        jnp.where(high, b, d),
    ]


def gather_line(own):
    near = flip(own, "col", 1)
    mid = lax.ppermute(own, "col", [(1, 2), (2, 1)])
    two_out = lax.ppermute(mid, "col", [(1, 0), (2, 3)])
    two_in = lax.ppermute(near, "col", [(1, 2), (2, 1)])
    three = lax.ppermute(two_in, "col", [(1, 0), (2, 3)])
    outer = (lax.axis_index("col") % 3) == 0
    return [own, near, jnp.where(outer, two_out, two_in), jnp.where(outer, three, mid)]


def scatter_line(parts):
    def plus(a, b):
        return (a.astype(jnp.float32) + b.astype(jnp.float32)).astype(jnp.bfloat16)

    far = lax.ppermute(parts[3], "col", [(0, 1), (3, 2)])
    second = plus(parts[2], far)
    out = lax.ppermute(second, "col", [(0, 1), (3, 2)])
    cross = lax.ppermute(second, "col", [(1, 2), (2, 1)])
    near = flip(plus(parts[1], cross), "col", 1)
    mid = lax.ppermute(plus(parts[3], out), "col", [(1, 2), (2, 1)])
    total = parts[0].astype(jnp.float32) + near.astype(jnp.float32) + mid.astype(jnp.float32)
    return total.astype(jnp.bfloat16)


def gather_heads(head_out):
    r, z = lax.axis_index("row"), lax.axis_index("col")
    if lax.axis_size("col") == 4:
        return xor_pick(gather_line(head_out), r ^ z)
    whole = lax.all_gather(head_out, "col", axis=1, tiled=True)
    width = whole.shape[1] // 4
    return [lax.dynamic_slice_in_dim(whole, (r ^ j) * width, width, 1) for j in range(4)]


def scatter_heads(parts):
    r, z = lax.axis_index("row"), lax.axis_index("col")
    if lax.axis_size("col") == 4:
        return scatter_line(xor_pick(parts, r ^ z))
    whole = jnp.concatenate(xor_pick(parts, r), axis=1).astype(jnp.float32)
    return lax.psum_scatter(whole, "col", scatter_dimension=1, tiled=True).astype(jnp.bfloat16)


def in_order(mine, other, axis):
    first = lax.axis_index("rep") == 0
    return jnp.where(
        first, jnp.concatenate([mine, other], axis), jnp.concatenate([other, mine], axis)
    )


def local(n_chunks, queries, key_vectors, value_vectors, cotangent, out_weight):
    tok_rows, features = queries.shape
    paired = lax.axis_size("rep") == 2
    me = lax.axis_index("rep")
    rows = out_weight.shape[0] // n_chunks
    width = features // n_chunks
    chunks = range(n_chunks)
    factor = float(tok_rows * lax.axis_size("row") * lax.axis_size("rep")) ** (-0.5)

    cot = jnp.concatenate([cotangent, flip(cotangent, "row", 2)], axis=0)
    weights, beside = [], []
    for h in chunks:
        block = lax.slice_in_dim(out_weight, h * rows, (h + 1) * rows, axis=0)
        if paired:
            half = flip(lax.dynamic_slice_in_dim(block, me * (rows // 2), rows // 2, 0), "row", 1)
            arrived = in_order(half, flip(half, "rep", 1), 0)
        else:
            arrived = flip(block, "row", 1)
        weights.append(block)
        beside.append(arrived)

    own, next_to = [], []
    for h in chunks:
        head_out = attention(queries, key_vectors, value_vectors, h * width, width)
        held = gather_heads(head_out)
        sent = flip(jnp.concatenate(held[2:], axis=1), "row", 2)
        own.append(jnp.concatenate([held[0], sent[:, :rows]], axis=0))
        next_to.append(jnp.concatenate([held[1], sent[:, rows:]], axis=0))

    grads = []
    for h in chunks:
        part = dot(cot, weights[h], NT).astype(jnp.bfloat16)
        part_beside = dot(cot, beside[h], NT).astype(jnp.bfloat16)
        sent = flip(
            jnp.concatenate([part[tok_rows:], part_beside[tok_rows:]], axis=1), "row", 2
        )
        summed = scatter_heads(
            [part[:tok_rows], part_beside[:tok_rows], sent[:, :rows], sent[:, rows:]]
        )
        grads = attention_grads(queries, key_vectors, value_vectors, summed, h * width, grads)

    grad_rows = []
    if paired:
        cot_both = jnp.concatenate([cot, flip(cot, "rep", 1)], axis=0)
    for h in chunks:
        if paired:
            half = rows // 2
            mine = [lax.dynamic_slice_in_dim(a, me * half, half, 1) for a in (own[h], next_to[h])]
            theirs = [
                lax.dynamic_slice_in_dim(a, (1 - me) * half, half, 1) for a in (own[h], next_to[h])
            ]
            got = flip(jnp.concatenate(theirs, axis=1), "rep", 1)
            left = jnp.concatenate([mine[0], got[:, :half]], axis=0)
            right = jnp.concatenate([mine[1], got[:, half:]], axis=0)
            away = flip(dot(right, cot_both, TN).astype(jnp.bfloat16), "row", 1)
            total = (dot(left, cot_both, TN) + away.astype(jnp.float32)) * factor
            total = total.astype(jnp.bfloat16)
            grad_rows.append(in_order(total, flip(total, "rep", 1), 0))
        else:
            away = flip(dot(next_to[h], cot, TN).astype(jnp.bfloat16), "row", 1)
            total = dot(own[h], cot, TN) + away.astype(jnp.float32)
            total = lax.psum(total.astype(jnp.bfloat16), "rep").astype(jnp.float32) * factor
            grad_rows.append(total.astype(jnp.bfloat16))
    grad_weight = jnp.concatenate(grad_rows, axis=0)

    every = jnp.concatenate([a for pair in zip(own, next_to) for a in pair], axis=1)
    every_weight = jnp.concatenate([a for pair in zip(weights, beside) for a in pair], axis=0)
    away = flip(dot(every[tok_rows:], every_weight).astype(jnp.bfloat16), "row", 2)
    projected = dot(every[:tok_rows], every_weight) + away.astype(jnp.float32)

    return (projected.astype(jnp.bfloat16), *grads, grad_weight)


def solution(mesh):
    placed = (P(("rep", "row"), "col"),) * 4 + (P("row", "col"),)
    n_chunks = 2 if mesh.shape["col"] == 4 else 1
    return jax.shard_map(
        functools.partial(local, n_chunks),
        mesh=mesh,
        in_specs=placed,
        out_specs=placed,
        check_vma=False,
    )
```

```python
import functools

import jax
import jax.numpy as jnp
from jax import lax
from jax.experimental import pallas as pl
from jax.experimental.pallas import tpu as pltpu
from jax.sharding import PartitionSpec as P

HSZ = 128
PATCH = 256
SCALE = HSZ ** (-0.5)
BF16, F32 = jnp.bfloat16, jnp.float32

NN = (((1,), (0,)), ((), ()))
NT = (((1,), (1,)), ((), ()))
TN = (((0,), (0,)), ((), ()))
VMEM = pl.BlockSpec(memory_space=pltpu.VMEM)
ANY = pl.BlockSpec(memory_space=pl.ANY)
HBM = pl.BlockSpec(memory_space=pltpu.HBM)
PARAMS = pltpu.CompilerParams(vmem_limit_bytes=40 * 2**20)


def dot(a, b, dims=NN):
    return lax.dot_general(a, b, dims, preferred_element_type=F32)


def cost(macs, moved, exps=0):
    return pl.CostEstimate(flops=2 * macs, bytes_accessed=moved, transcendentals=exps)


def like(shape, dtype=BF16):
    return jax.ShapeDtypeStruct(shape, dtype)


def call(kernel, arrays, in_specs, after, prefetch=0, **options):
    n = len(arrays)

    def body(*refs):
        kernel(*refs[:n], *refs[n + len(after) :])

    in_specs = list(in_specs) + [ANY] * len(after)
    if prefetch:
        options["grid_spec"] = pltpu.PrefetchScalarGridSpec(
            num_scalar_prefetch=prefetch,
            grid=options.pop("grid"),
            in_specs=in_specs,
            out_specs=options.pop("out_specs"),
        )
    else:
        options["in_specs"] = in_specs
    return pl.pallas_call(body, compiler_params=PARAMS, **options)(*arrays, *after)


def position():
    z = lax.axis_index("col")
    return lax.axis_index("row") ^ z, lax.axis_index("rep"), lax.rem(z, 3) == 0


def tie(x, after):
    return call(
        lambda *refs: None,
        (x,),
        [ANY],
        after,
        out_specs=ANY,
        out_shape=like(x.shape, x.dtype),
        input_output_aliases={0: 0},
        cost_estimate=cost(0, 0),
        name="tie",
    )


def plus_kernel(a_ref, b_ref, out_ref):
    out_ref[...] = (a_ref[...].astype(F32) + b_ref[...].astype(F32)).astype(out_ref.dtype)


def plus(a, b, after=()):
    spec = pl.BlockSpec(a.shape, lambda i: (0, 0))
    return call(
        plus_kernel,
        (a, b),
        [spec] * 2,
        after,
        grid=(1,),
        out_specs=spec,
        out_shape=like(a.shape),
        cost_estimate=cost(0, 6 * a.size),
        name="plus",
    )


def copies(pairs, sems):
    started = [pltpu.make_async_copy(a, b, sems.at[i]) for i, (a, b) in enumerate(pairs)]
    for copy in started:
        copy.start()
    return started


def softmax_t(q, k):
    scores = dot(k, q, NT)
    lifted = jnp.exp((scores - jnp.max(scores, axis=0, keepdims=True)) * SCALE)
    return lifted * (1.0 / jnp.sum(lifted, axis=0, keepdims=True))


def forward_kernel(q_ref, k_ref, v_ref, o_ref):
    for lo in range(0, q_ref.shape[1], HSZ):
        cols = slice(lo, lo + HSZ)
        prob = softmax_t(q_ref[:, cols], k_ref[:, cols]).astype(BF16)
        o_ref[:, cols] = dot(prob, v_ref[:, cols], TN).astype(BF16)


def backward_head(q, k, v, g):
    prob = softmax_t(q, k)
    grad_prob = dot(v, g, NT)
    delta = jnp.sum(prob * grad_prob, axis=0, keepdims=True)
    grad_score = (prob * (grad_prob - delta) * SCALE).astype(BF16)
    return (
        dot(grad_score, k, TN).astype(BF16),
        dot(grad_score, q).astype(BF16),
        dot(prob.astype(BF16), g).astype(BF16),
    )


def backward_kernel(q_ref, k_ref, v_ref, g_ref, *grads):
    for lo in range(0, q_ref.shape[1], HSZ):
        cols = slice(lo, lo + HSZ)
        got = backward_head(q_ref[:, cols], k_ref[:, cols], v_ref[:, cols], g_ref[:, cols])
        for ref, value in zip(grads, got):
            ref[:, cols] = value


def backward_sum_kernel(at, q_ref, k_ref, v_ref, *refs):
    outs, (gq, gk, gv, sems) = refs[-7:-4], refs[-4:]
    for lo in range(0, q_ref.shape[1], HSZ):
        cols = slice(lo, lo + HSZ)
        g = sum(ref[:, cols].astype(F32) for ref in refs[:4]).astype(BF16)
        got = backward_head(q_ref[:, cols], k_ref[:, cols], v_ref[:, cols], g)
        for ref, value in zip((gq, gk, gv), got):
            ref[:, cols] = value
    stores = [(a, out.at[:, pl.ds(at, a.shape[1])]) for a, out in zip((gq, gk, gv), outs)]
    for copy in copies(stores, sems):
        copy.wait()


def head_width(width):
    return (2 if width % (2 * HSZ) == 0 else 1) * HSZ


def attention(q, k, v, at, width, after=()):
    wide = head_width(width)
    spec = pl.BlockSpec((PATCH, wide), lambda i, h: (i, h + at // wide))
    tokens = q.shape[0]
    return call(
        forward_kernel,
        (q, k, v),
        [spec] * 3,
        after,
        grid=(tokens // PATCH, width // wide),
        out_specs=pl.BlockSpec((PATCH, wide), lambda i, h: (i, h)),
        out_shape=like((tokens, width)),
        cost_estimate=cost(2 * tokens * PATCH * width, 8 * tokens * width),
        name="attention",
    )


def attention_grads(q, k, v, g):
    wide = head_width(q.shape[1])
    spec = pl.BlockSpec((PATCH, wide), lambda i, h: (i, h))
    tokens, width = q.shape
    return pl.pallas_call(
        backward_kernel,
        grid=(tokens // PATCH, width // wide),
        in_specs=[spec] * 4,
        out_specs=[spec] * 3,
        out_shape=[like(q.shape)] * 3,
        cost_estimate=cost(5 * tokens * PATCH * width, 14 * tokens * width),
        name="attention_grads",
    )(q, k, v, g)


def attention_grads_sum(q, k, v, terms, h, before, after):
    tokens, width = terms[0].shape
    spec = pl.BlockSpec((tokens, width), lambda i: (0, h))
    part = pl.BlockSpec((tokens, width), lambda i: (0, 0))
    return call(
        functools.partial(backward_sum_kernel, h * width),
        (q, k, v, *terms, *before),
        [spec] * 3 + [part] * 4 + [HBM] * len(before),
        after,
        grid=(1,),
        out_specs=[HBM] * 3,
        out_shape=[like(q.shape)] * 3,
        scratch_shapes=[pltpu.VMEM((tokens, width), BF16)] * 3 + [pltpu.SemaphoreType.DMA((3,))],
        input_output_aliases={7 + i: i for i in range(len(before))},
        cost_estimate=cost(5 * tokens * PATCH * width, 20 * tokens * width),
        name="attention_grads",
    )


def fetch_halves_kernel(weight_ref, *refs):
    outs, sems = refs[:-1], refs[-1]
    half, me = outs[0].shape[0], position()[1]
    for copy in copies(
        [
            (weight_ref.at[pl.ds(pl.multiple_of((2 * h + me) * half, half), half)], out)
            for h, out in enumerate(outs)
        ],
        sems,
    ):
        copy.wait()


def fetch_halves(weight):
    rows, depth = weight.shape
    return call(
        fetch_halves_kernel,
        (weight,),
        [HBM],
        (),
        out_specs=[ANY] * 2,
        out_shape=[like((rows // 4, depth))] * 2,
        scratch_shapes=[pltpu.SemaphoreType.DMA((2,))],
        cost_estimate=cost(0, 2 * rows * depth),
        name="fetch_halves",
    )


def route_heads_kernel(*refs):
    m = position()[0]
    sources, (keep_ref, send_ref, sems) = refs[:4], refs[4:]
    targets = [keep_ref.at[0], keep_ref.at[1], send_ref.at[0], send_ref.at[1]]
    for j, target in enumerate(targets):
        for step, source in enumerate(sources):

            @pl.when((m ^ j) == step)
            def _(target=target, j=j, source=source):
                pltpu.make_async_copy(source, target, sems.at[j]).start()

    for j, target in enumerate(targets):
        pltpu.make_async_copy(sources[0], target, sems.at[j]).wait()


def route_heads(sources, after):
    shape = (2, *sources[0].shape)
    return call(
        route_heads_kernel,
        sources,
        [ANY] * 4,
        after,
        out_specs=[ANY] * 2,
        out_shape=[like(shape)] * 2,
        scratch_shapes=[pltpu.SemaphoreType.DMA((4,))],
        cost_estimate=cost(0, 16 * sources[0].size),
        name="route_heads",
    )


def head_parts_kernel(at, cot_ref, far_ref, mine_ref, other_ref, w_ref, keep_ref, send_ref, w, sems):
    (load,) = copies([(w_ref.at[pl.ds(at, w.shape[0])], w)], sems)
    m, me, _ = position()
    low, half = m & 1, mine_ref.shape[0]
    sides = ((far_ref, send_ref), (cot_ref, keep_ref))
    for source, target in sides:
        for ref, i in ((mine_ref, me), (other_ref, 1 - me)):
            cols = pl.ds(pl.multiple_of(i * half, half), half)
            target[1 - low, :, cols] = dot(source[...], ref[...], NT).astype(BF16)
    load.wait()
    for source, target in sides:
        target[low] = dot(source[...], w[...], NT).astype(BF16)


def head_parts(cot, cot_far, weight, mine, other, h, after):
    tokens, depth = cot.shape
    rows = 2 * mine.shape[0]
    whole = lambda a: pl.BlockSpec(a.shape, lambda i: (0, 0))
    out = pl.BlockSpec((2, tokens, rows), lambda i: (0, 0, 0))
    return call(
        functools.partial(head_parts_kernel, h * rows),
        (cot, cot_far, mine, other, weight),
        [whole(cot)] * 2 + [whole(mine)] * 2 + [HBM],
        after,
        grid=(1,),
        out_specs=[out] * 2,
        out_shape=[like((2, tokens, rows))] * 2,
        scratch_shapes=[pltpu.VMEM((rows, depth), BF16), pltpu.SemaphoreType.DMA((1,))],
        cost_estimate=cost(4 * tokens * depth * rows, 4 * (tokens + rows) * depth + 8 * tokens * rows),
        name="head_parts",
    )


def route_parts_kernel(keep_ref, recv_ref, *refs):
    targets, sems = refs[:4], refs[4]
    m = position()[0]
    for step, target in enumerate(targets):
        for high, source in ((step >> 1, keep_ref), (1 - (step >> 1), recv_ref)):

            @pl.when(m >> 1 == high)
            def _(target=target, step=step, source=source):
                pltpu.make_async_copy(source.at[step & 1], target, sems.at[step]).start()

    for step, target in enumerate(targets):
        pltpu.make_async_copy(keep_ref.at[0], target, sems.at[step]).wait()


def route_parts(keep, recv, after):
    shape = keep.shape[1:]
    return call(
        route_parts_kernel,
        (keep, recv),
        [ANY] * 2,
        after,
        out_specs=[ANY] * 4,
        out_shape=[like(shape)] * 4,
        scratch_shapes=[pltpu.SemaphoreType.DMA((4,))],
        cost_estimate=cost(0, 8 * keep.size),
        name="route_parts",
    )


def weight_parts_kernel(*refs):
    heads, cots, (away_ref, own_ref) = refs[:4], refs[4:8], refs[8:]
    half, me = heads[0].shape[2] // 2, position()[1]
    cols = pl.ds(pl.multiple_of(me * half, half), half)
    for j, target in ((1, away_ref), (0, own_ref)):
        left = jnp.concatenate([ref[j, :, cols] for ref in heads], axis=0)
        right = jnp.concatenate([ref[...] for ref in cots], axis=0)
        target[...] = dot(left, right, TN).astype(target.dtype)


def weight_parts(heads, cots, after):
    _, tokens, rows = heads[0].shape
    depth = cots[0].shape[1]
    wide = depth // 3 if depth % 384 == 0 else depth
    whole = pl.BlockSpec(heads[0].shape, lambda i: (0, 0, 0))
    cot = pl.BlockSpec((tokens, wide), lambda i: (0, i))
    out = pl.BlockSpec((rows // 2, wide), lambda i: (0, i))
    return call(
        weight_parts_kernel,
        (*heads, *cots),
        [whole] * 4 + [cot] * 4,
        after,
        grid=(depth // wide,),
        out_specs=[out] * 2,
        out_shape=[like((rows // 2, depth)), like((rows // 2, depth), F32)],
        cost_estimate=cost(4 * tokens * rows * depth, 16 * tokens * rows + 8 * tokens * depth + 3 * rows * depth),
        name="weight_parts",
    )


def weight_total(own, away, factor, h, before, rows, after):
    half, depth = own.shape

    def kernel(own_ref, away_ref, *refs):
        *_, total_ref, out_ref, own, away, total, sems = refs
        me = position()[1]
        at = pl.multiple_of((2 * h + me) * half, half)
        for copy in copies([(own_ref, own), (away_ref, away)], sems):
            copy.wait()
        total[...] = ((own[...] + away[...].astype(F32)) * factor).astype(BF16)
        for copy in copies([(total, total_ref), (total, out_ref.at[pl.ds(at, half)])], sems):
            copy.wait()

    return call(
        kernel,
        (own, away, *before),
        [ANY] * (2 + len(before)),
        after,
        out_specs=[ANY] * 2,
        out_shape=[like((half, depth)), like((rows, depth))],
        scratch_shapes=[
            pltpu.VMEM((half, depth), F32),
            pltpu.VMEM((half, depth), BF16),
            pltpu.VMEM((half, depth), BF16),
            pltpu.SemaphoreType.DMA((2,)),
        ],
        input_output_aliases={2: 1} if before else {},
        cost_estimate=cost(0, 10 * half * depth),
        name="weight_total",
    )


def weight_fill_kernel(first_ref, second_ref, held_ref, out_ref, sems):
    half, me = first_ref.shape[0], position()[1]
    for copy in copies(
        [
            (ref, out_ref.at[pl.ds(pl.multiple_of((2 * h + 1 - me) * half, half), half)])
            for h, ref in enumerate((first_ref, second_ref))
        ],
        sems,
    ):
        copy.wait()


def weight_fill(first, second, held, after=()):
    return call(
        weight_fill_kernel,
        (first, second, held),
        [ANY] * 3,
        after,
        out_specs=ANY,
        out_shape=like(held.shape),
        scratch_shapes=[pltpu.SemaphoreType.DMA((2,))],
        input_output_aliases={2: 0},
        cost_estimate=cost(0, 8 * first.size),
        name="weight_fill",
    )


def project_kernel(*refs):
    heads, besides, weight_ref, out_ref, weight, total, sems = refs[:2], refs[2:6], *refs[6:]
    (load,) = copies([(weight_ref, weight)], sems)
    me = position()[1]
    rows, half = heads[0].shape[2], besides[0].shape[0]
    for h in (0, 1):
        for ref, at in ((besides[2 * h], me), (besides[2 * h + 1], 1 - me)):
            cols = pl.ds(pl.multiple_of(at * half, half), half)
            term = dot(heads[h][1, :, cols], ref[...])
            total[...] = term if h == 0 and at is me else total[...] + term
    load.wait()
    for h in (0, 1):
        total[...] += dot(heads[h][0], weight[h * rows : (h + 1) * rows, :])
    out_ref[...] = total[...].astype(out_ref.dtype)


def project(heads, weight, besides, dtype, after):
    _, tokens, _ = heads[0].shape
    rows, depth = weight.shape
    whole = lambda a: pl.BlockSpec(a.shape, lambda i: (0,) * a.ndim)
    return call(
        project_kernel,
        (*heads, *besides, weight),
        [whole(a) for a in (*heads, *besides)] + [HBM],
        after,
        grid=(1,),
        out_specs=pl.BlockSpec((tokens, depth), lambda i: (0, 0)),
        out_shape=like((tokens, depth), dtype),
        scratch_shapes=[
            pltpu.VMEM((rows, depth), BF16),
            pltpu.VMEM((tokens, depth), F32),
            pltpu.SemaphoreType.DMA((1,)),
        ],
        cost_estimate=cost(2 * tokens * rows * depth, 4 * (tokens + rows) * depth),
        name="project",
    )


def flip(x, axis, bit):
    return lax.ppermute(x, axis, [(i, i ^ bit) for i in range(lax.axis_size(axis))])


def local_grid(queries, key_vectors, value_vectors, cotangent, out_weight):
    tok_rows, features = queries.shape
    width = features // 2
    factor = float(tok_rows * lax.axis_size("row") * lax.axis_size("rep")) ** (-0.5)
    rows = out_weight.shape[0]

    def grads(terms, h, before, after):
        return attention_grads_sum(queries, key_vectors, value_vectors, terms, h, before, after)

    def parts(h, beside, after):
        return head_parts(cotangent, cot_far, out_weight, *beside, h, after)

    def across(blocks):
        return flip(blocks[3], "col", 3), flip(blocks[1], "col", 1), flip(blocks[2], "col", 2)

    halves = fetch_halves(out_weight)
    cot_far = flip(cotangent, "row", 2)
    mine0, mine1 = [flip(a, "row", 1) for a in halves]
    own0 = attention(queries, key_vectors, value_vectors, 0, width, halves)
    own1 = attention(queries, key_vectors, value_vectors, width, width, [own0])
    three, one, two = across([own0] * 4)

    held0, send_h0 = route_heads((own0, one, two, three), [own1])
    got_h0 = flip(send_h0, "row", 2)
    own1 = tie(own1, [held0])
    three, one, two = across([own1] * 4)
    mine0 = tie(mine0, [cot_far, held0])
    beside0 = (mine0, flip(mine0, "rep", 1))
    held0_core = flip(held0, "rep", 1)
    keep0, send0 = parts(0, beside0, [held0])
    cots = [cotangent, cot_far, flip(cotangent, "rep", 1), flip(tie(cot_far, [held0]), "rep", 1)]

    got_h0 = tie(got_h0, [send0, three, one])
    got0 = flip(tie(send0, [got_h0]), "row", 2)
    mine1 = tie(mine1, [got_h0])
    beside1 = (mine1, flip(mine1, "rep", 1))
    heads0 = [held0, got_h0, held0_core, flip(got_h0, "rep", 1)]
    away0, total0 = weight_parts(heads0, cots, [mine1])
    away0 = flip(away0, "row", 1)
    keep1, send1 = parts(1, beside1, [total0])

    got0 = tie(got0, [send1])
    held1, send_h1 = route_heads((own1, one, two, three), [got0])
    got_h1 = flip(send_h1, "row", 2)
    terms0 = route_parts(keep0, got0, [held1])
    three, one, two = across(terms0)
    held1_core = flip(held1, "rep", 1)

    got_h1 = tie(got_h1, [three, one])
    got1 = flip(tie(send1, [got_h1]), "row", 2)
    heads1 = [held1, got_h1, held1_core, flip(got_h1, "rep", 1)]
    total0, held = weight_total(total0, away0, factor, 0, (), rows, [got_h1])
    total0 = flip(total0, "rep", 1)
    away1, total1 = weight_parts(heads1, cots, [held])
    away1 = flip(away1, "row", 1)
    besides = [*beside0, *beside1]
    sent = project([got_h0, got_h1], out_weight, besides, BF16, [total1])

    got1 = tie(got1, [sent, two])
    terms1 = route_parts(keep1, got1, [sent])
    from_far = flip(tie(sent, [terms1[0]]), "row", 2)
    some = grads((terms0[0], one, two, three), 0, (), [terms1[0]])
    three, one, _ = across(terms1)
    projected = project([held0, held1], out_weight, besides, F32, [some[0]])
    two = flip(tie(terms1[2], [three, one]), "col", 2)

    away1 = tie(away1, [projected, three, one])
    total1, held = weight_total(total1, away1, factor, 1, (held,), rows, [projected])
    grad_weight = weight_fill(total0, flip(total1, "rep", 1), held)
    projected = plus(projected, from_far, [held])
    full = grads((terms1[0], one, two, three), 1, some, [projected])
    return (projected, *full, grad_weight)


def local_any(queries, key_vectors, value_vectors, cotangent, out_weight):
    tok_rows, features = queries.shape
    rows = out_weight.shape[0]
    r = lax.axis_index("row")
    cot = jnp.concatenate([cotangent, flip(cotangent, "row", 2)], axis=0)
    beside = flip(out_weight, "row", 1)

    head_out = attention(queries, key_vectors, value_vectors, 0, features)
    whole = lax.all_gather(head_out, "col", axis=1, tiled=True)
    held = [lax.dynamic_slice_in_dim(whole, (r ^ j) * rows, rows, 1) for j in range(4)]
    sent = flip(jnp.concatenate(held[2:], axis=1), "row", 2)
    own = jnp.concatenate([held[0], sent[:, :rows]], axis=0)
    next_to = jnp.concatenate([held[1], sent[:, rows:]], axis=0)

    part, part_beside = dot(cot, out_weight, NT), dot(cot, beside, NT)
    sent = flip(
        jnp.concatenate([part[tok_rows:], part_beside[tok_rows:]], axis=1).astype(BF16), "row", 2
    ).astype(F32)
    parts = jnp.stack([part[:tok_rows], part_beside[:tok_rows], sent[:, :rows], sent[:, rows:]])
    whole = jnp.concatenate([parts[r ^ j] for j in range(4)], axis=1)
    summed = lax.psum_scatter(whole, "col", scatter_dimension=1, tiled=True)
    grads = attention_grads(queries, key_vectors, value_vectors, summed.astype(BF16))

    factor = float(tok_rows * lax.axis_size("row") * lax.axis_size("rep")) ** (-0.5)
    away = flip(dot(next_to, cot, TN).astype(BF16), "row", 1)
    total = dot(own, cot, TN) + away.astype(F32)
    total = lax.psum(total.astype(BF16), "rep").astype(F32) * factor

    away = dot(own[tok_rows:], out_weight) + dot(next_to[tok_rows:], beside)
    away = flip(away.astype(BF16), "row", 2)
    projected = dot(own[:tok_rows], out_weight) + dot(next_to[:tok_rows], beside)
    projected = projected + away.astype(F32)
    return (projected.astype(BF16), *grads, total.astype(BF16))


def solution(mesh):
    placed = (P(("rep", "row"), "col"),) * 4 + (P("row", "col"),)
    grid = mesh.shape["col"] == 4 and mesh.shape["rep"] == 2
    return jax.shard_map(
        local_grid if grid else local_any,
        mesh=mesh,
        in_specs=placed,
        out_specs=placed,
        check_vma=False,
    )
```

```python
import functools

import jax
import jax.numpy as jnp
from jax import lax
from jax.experimental import pallas as pl
from jax.experimental.pallas import tpu as pltpu
from jax.sharding import PartitionSpec as P

HSZ = 128
PATCH = 256
SCALE = HSZ ** (-0.5)
BF16, F32 = jnp.bfloat16, jnp.float32

NN = (((1,), (0,)), ((), ()))
NT = (((1,), (1,)), ((), ()))
TN = (((0,), (0,)), ((), ()))
VMEM = pl.BlockSpec(memory_space=pltpu.VMEM)
ANY = pl.BlockSpec(memory_space=pl.ANY)
HBM = pl.BlockSpec(memory_space=pltpu.HBM)
PARAMS = pltpu.CompilerParams(vmem_limit_bytes=24 * 2**20)


def dot(a, b, dims=NN):
    return lax.dot_general(a, b, dims, preferred_element_type=F32)


def cost(macs, moved, exps=0):
    return pl.CostEstimate(flops=2 * macs, bytes_accessed=moved, transcendentals=exps)


def like(shape, dtype=BF16):
    return jax.ShapeDtypeStruct(shape, dtype)


def call(kernel, arrays, in_specs, after, out_specs, out_shape, **options):
    n, many = len(arrays), isinstance(out_shape, list)
    shapes, specs = (out_shape, out_specs) if many else ([out_shape], [out_specs])
    first = n + len(after)

    def body(*refs):
        kernel(*refs[:n], *refs[first : first + len(shapes)], *refs[first + len(shapes) + 1 :])

    *outs, mark = pl.pallas_call(
        body,
        in_specs=[*in_specs, *[ANY] * len(after)],
        out_specs=[*specs, ANY],
        out_shape=[*shapes, like((8, 128), F32)],
        compiler_params=PARAMS,
        **options,
    )(*arrays, *after)
    return (outs if many else outs[0]), mark


def tie(x, *after):
    return call(
        lambda *refs: None,
        (x,),
        [ANY],
        after,
        ANY,
        like(x.shape, x.dtype),
        input_output_aliases={0: 0},
        cost_estimate=cost(0, 0),
        name="tie",
    )[0]


def position():
    z = lax.axis_index("col")
    return lax.axis_index("row") ^ z, lax.axis_index("rep"), lax.rem(z, 3) == 0


def plus_kernel(a_ref, b_ref, out_ref):
    out_ref[...] = (a_ref[...].astype(F32) + b_ref[...].astype(F32)).astype(out_ref.dtype)


def plus(a, b, after=()):
    spec = pl.BlockSpec(a.shape, lambda i: (0, 0))
    return call(
        plus_kernel,
        (a, b),
        [spec] * 2,
        after,
        grid=(1,),
        out_specs=spec,
        out_shape=like(a.shape),
        cost_estimate=cost(0, 6 * a.size),
        name="plus",
    )


def copies(pairs, sems):
    started = [pltpu.make_async_copy(a, b, sems.at[i]) for i, (a, b) in enumerate(pairs)]
    for copy in started:
        copy.start()
    return started


def softmax_t(q, k):
    scores = dot(k, q, NT)
    lifted = jnp.exp((scores - jnp.max(scores, axis=0, keepdims=True)) * SCALE)
    return lifted * (1.0 / jnp.sum(lifted, axis=0, keepdims=True))


def forward_kernel(q_ref, k_ref, v_ref, o_ref):
    for lo in range(0, q_ref.shape[1], HSZ):
        cols = slice(lo, lo + HSZ)
        prob = softmax_t(q_ref[:, cols], k_ref[:, cols]).astype(BF16)
        o_ref[:, cols] = dot(prob, v_ref[:, cols], TN).astype(BF16)


def backward_head(q, k, v, g):
    prob = softmax_t(q, k)
    grad_prob = dot(v, g, NT)
    delta = jnp.sum(prob * grad_prob, axis=0, keepdims=True)
    grad_score = (prob * (grad_prob - delta) * SCALE).astype(BF16)
    return (
        dot(grad_score, k, TN).astype(BF16),
        dot(grad_score, q).astype(BF16),
        dot(prob.astype(BF16), g).astype(BF16),
    )


def backward_kernel(q_ref, k_ref, v_ref, g_ref, *grads):
    for lo in range(0, q_ref.shape[1], HSZ):
        cols = slice(lo, lo + HSZ)
        got = backward_head(q_ref[:, cols], k_ref[:, cols], v_ref[:, cols], g_ref[:, cols])
        for ref, value in zip(grads, got):
            ref[:, cols] = value


def backward_sum_kernel(q_ref, k_ref, v_ref, *refs):
    for lo in range(0, q_ref.shape[1], HSZ):
        cols = slice(lo, lo + HSZ)
        g = sum(ref[:, cols].astype(F32) for ref in refs[:-3]).astype(BF16)
        got = backward_head(q_ref[:, cols], k_ref[:, cols], v_ref[:, cols], g)
        for ref, value in zip(refs[-3:], got):
            ref[:, cols] = value


def head_width(width):
    return (2 if width % (2 * HSZ) == 0 else 1) * HSZ


def attention(q, k, v, at, width, after=()):
    wide = head_width(width)
    spec = pl.BlockSpec((PATCH, wide), lambda i, h: (i, h + at // wide))
    tokens = q.shape[0]
    return call(
        forward_kernel,
        (q, k, v),
        [spec] * 3,
        after,
        grid=(tokens // PATCH, width // wide),
        out_specs=pl.BlockSpec((PATCH, wide), lambda i, h: (i, h)),
        out_shape=like((tokens, width)),
        cost_estimate=cost(2 * tokens * PATCH * width, 8 * tokens * width),
        name="attention",
    )


def attention_grads(q, k, v, g):
    wide = head_width(q.shape[1])
    spec = pl.BlockSpec((PATCH, wide), lambda i, h: (i, h))
    tokens, width = q.shape
    return pl.pallas_call(
        backward_kernel,
        grid=(tokens // PATCH, width // wide),
        in_specs=[spec] * 4,
        out_specs=[spec] * 3,
        out_shape=[like(q.shape)] * 3,
        cost_estimate=cost(5 * tokens * PATCH * width, 14 * tokens * width),
        name="attention_grads",
    )(q, k, v, g)


def attention_grads_sum(q, k, v, terms, after):
    tokens, width = q.shape
    wide = head_width(width)
    spec = pl.BlockSpec((PATCH, wide), lambda i, h: (i, h))
    return call(
        backward_sum_kernel,
        (q, k, v, *terms),
        [spec] * (3 + len(terms)),
        after,
        grid=(tokens // PATCH, width // wide),
        out_specs=[spec] * 3,
        out_shape=[like(q.shape)] * 3,
        cost_estimate=cost(5 * tokens * PATCH * width, 18 * tokens * width),
        name="attention_grads",
    )


def fetch_halves_kernel(weight_ref, *refs):
    outs, sems = refs[:-1], refs[-1]
    half, me = outs[0].shape[0], position()[1]
    for copy in copies(
        [
            (weight_ref.at[pl.ds(pl.multiple_of((2 * h + me) * half, half), half)], out)
            for h, out in enumerate(outs)
        ],
        sems,
    ):
        copy.wait()


def fetch_halves(weight, after):
    rows, depth = weight.shape
    return call(
        fetch_halves_kernel,
        (weight,),
        [HBM],
        after,
        out_specs=[ANY] * 2,
        out_shape=[like((rows // 4, depth))] * 2,
        scratch_shapes=[pltpu.SemaphoreType.DMA((2,))],
        cost_estimate=cost(0, 2 * rows * depth),
        name="fetch_halves",
    )


def route_heads_kernel(*refs):
    m, _, outer = position()
    sources, (keep_ref, two_ref, three_ref, sems) = refs[:6], refs[6:]
    steps = ((0, None), (1, None), (2, True), (2, False), (3, True), (3, False))
    targets = [keep_ref.at[0], keep_ref.at[1], two_ref, three_ref]
    for j, target in enumerate(targets):
        for source, (step, at_ends) in zip(sources, steps):
            here = (m ^ j) == step

            @pl.when(here if at_ends is None else here & (outer == at_ends))
            def _(target=target, j=j, source=source):
                pltpu.make_async_copy(source, target, sems.at[j]).start()

    for j, target in enumerate(targets):
        pltpu.make_async_copy(sources[0], target, sems.at[j]).wait()


def route_heads(sources, after):
    shape = sources[0].shape
    return call(
        route_heads_kernel,
        sources,
        [ANY] * 6,
        after,
        out_specs=[ANY] * 3,
        out_shape=[like((2, *shape)), like(shape), like(shape)],
        scratch_shapes=[pltpu.SemaphoreType.DMA((4,))],
        cost_estimate=cost(0, 16 * sources[0].size),
        name="route_heads",
    )


def head_parts_kernel(at, cot_ref, far_ref, mine_ref, other_ref, w_ref, keep_ref, send_ref, w, sems):
    (load,) = copies([(w_ref.at[pl.ds(at, w.shape[0])], w)], sems)
    m, me, _ = position()
    low, half = m & 1, mine_ref.shape[0]
    sides = ((far_ref, send_ref), (cot_ref, keep_ref))
    for source, target in sides:
        for ref, i in ((mine_ref, me), (other_ref, 1 - me)):
            cols = pl.ds(pl.multiple_of(i * half, half), half)
            target[1 - low, :, cols] = dot(source[...], ref[...], NT).astype(BF16)
    load.wait()
    for source, target in sides:
        target[low] = dot(source[...], w[...], NT).astype(BF16)


def head_parts(cot, cot_far, weight, mine, other, h, after):
    tokens, depth = cot.shape
    rows = 2 * mine.shape[0]
    whole = lambda a: pl.BlockSpec(a.shape, lambda i: (0, 0))
    out = pl.BlockSpec((2, tokens, rows), lambda i: (0, 0, 0))
    return call(
        functools.partial(head_parts_kernel, h * rows),
        (cot, cot_far, mine, other, weight),
        [whole(cot)] * 2 + [whole(mine)] * 2 + [HBM],
        after,
        grid=(1,),
        out_specs=[out] * 2,
        out_shape=[like((2, tokens, rows))] * 2,
        scratch_shapes=[pltpu.VMEM((rows, depth), BF16), pltpu.SemaphoreType.DMA((1,))],
        cost_estimate=cost(4 * tokens * depth * rows, 4 * (tokens + rows) * depth + 8 * tokens * rows),
        name="head_parts",
    )


def route_parts_kernel(*refs):
    parts, targets, sems = refs[:4], refs[4:8], refs[8]
    m = position()[0]
    width = parts[0].shape[2]
    views = [target.at[:, pl.ds(h * width, width)] for target in targets for h in (0, 1)]
    for i, view in enumerate(views):
        step, h = i // 2, i % 2
        for high, source in ((step >> 1, parts[2 * h]), (1 - (step >> 1), parts[2 * h + 1])):

            @pl.when(m >> 1 == high)
            def _(view=view, i=i, source=source.at[step & 1]):
                pltpu.make_async_copy(source, view, sems.at[i]).start()

    for i, view in enumerate(views):
        pltpu.make_async_copy(parts[0].at[0], view, sems.at[i]).wait()


def route_parts(parts, after):
    _, tokens, width = parts[0].shape
    return call(
        route_parts_kernel,
        parts,
        [ANY] * 4,
        after,
        out_specs=[ANY] * 4,
        out_shape=[like((tokens, 2 * width))] * 4,
        scratch_shapes=[pltpu.SemaphoreType.DMA((8,))],
        cost_estimate=cost(0, 16 * parts[0].size),
        name="route_parts",
    )


def weight_parts_kernel(*refs):
    heads, cots, out_ref = refs[:4], refs[4:8], refs[8]
    half = out_ref.shape[0]
    cols = pl.ds(pl.multiple_of(position()[1] * half, half), half)
    left = jnp.concatenate([ref.at[0][:, cols] if len(ref.shape) == 3 else ref[:, cols] for ref in heads], axis=0)
    right = jnp.concatenate([ref[...] for ref in cots], axis=0)
    out_ref[...] = dot(left, right, TN).astype(out_ref.dtype)


def weight_parts(j, heads, cots, dtype, after):
    tokens, rows = heads[1].shape
    depth = cots[0].shape[1]
    wide = depth // 3 if depth % 384 == 0 else depth
    pair = pl.BlockSpec((1, tokens, rows), lambda i: (j, 0, 0))
    whole = pl.BlockSpec((tokens, rows), lambda i: (0, 0))
    return call(
        weight_parts_kernel,
        (*heads, *cots),
        [pair, whole] * 2 + [pl.BlockSpec((tokens, wide), lambda i: (0, i))] * 4,
        after,
        grid=(depth // wide,),
        out_specs=pl.BlockSpec((rows // 2, wide), lambda i: (0, i)),
        out_shape=like((rows // 2, depth), dtype),
        cost_estimate=cost(2 * tokens * rows * depth, 8 * tokens * (rows + depth) + rows * depth),
        name="weight_parts",
    )


def weight_total(own, away, factor, rows, after):
    half, depth = own.shape
    cut = half // 2

    def kernel(own_ref, away_ref, total_ref, out_ref, own, away, total, sems):
        at = position()[1] * half
        loads, stores = [], []
        for i in (0, 1):
            part = pl.ds(i * cut, cut)
            loads.append(
                copies([(own_ref.at[part], own.at[part]), (away_ref.at[part], away.at[part])], sems.at[i])
            )
        for i, load in enumerate(loads):
            part = pl.ds(i * cut, cut)
            for copy in load:
                copy.wait()
            total[part] = ((own[part] + away[part].astype(F32)) * factor).astype(BF16)
            place = out_ref.at[pl.ds(pl.multiple_of(at + i * cut, cut), cut)]
            stores += copies([(total.at[part], total_ref.at[part]), (total.at[part], place)], sems.at[2 + i])
        for copy in stores:
            copy.wait()

    return call(
        kernel,
        (own, away),
        [ANY] * 2,
        after,
        out_specs=[ANY] * 2,
        out_shape=[like((half, depth)), like((rows, depth))],
        scratch_shapes=[
            pltpu.VMEM((half, depth), F32),
            pltpu.VMEM((half, depth), BF16),
            pltpu.VMEM((half, depth), BF16),
            pltpu.SemaphoreType.DMA((4, 2)),
        ],
        cost_estimate=cost(0, 10 * half * depth),
        name="weight_total",
    )


def weight_fill_kernel(other_ref, held_ref, out_ref, sems):
    half = other_ref.shape[0]
    at = pl.multiple_of((1 - position()[1]) * half, half)
    for copy in copies([(other_ref, out_ref.at[pl.ds(at, half)])], sems):
        copy.wait()


def weight_fill(other, held, after=()):
    return call(
        weight_fill_kernel,
        (other, held),
        [ANY] * 2,
        after,
        out_specs=ANY,
        out_shape=like(held.shape),
        scratch_shapes=[pltpu.SemaphoreType.DMA((1,))],
        input_output_aliases={1: 0},
        cost_estimate=cost(0, 4 * other.size),
        name="weight_fill",
    )


def project_kernel(own_ref, beside_ref, *refs):
    besides, weight_ref, out_ref, weight, total, sems = refs[:4], *refs[4:]
    (load,) = copies([(weight_ref, weight)], sems)
    me = position()[1]
    half = besides[0].shape[0]
    for i, ref in enumerate(besides):
        at = i // 2 * 2 + (1 - me if i % 2 else me)
        cols = pl.ds(pl.multiple_of(at * half, half), half)
        block = beside_ref[0, :, cols] if len(beside_ref.shape) == 3 else beside_ref[:, cols]
        term = dot(block, ref[...])
        total[...] = term if i == 0 else total[...] + term
    load.wait()
    total[...] += dot(own_ref[0] if len(own_ref.shape) == 3 else own_ref[...], weight[...])
    out_ref[...] = total[...].astype(out_ref.dtype)


def project(heads, weight, besides, dtype, after):
    rows, depth = weight.shape
    tokens = heads[0].shape[-2]
    whole = lambda a: pl.BlockSpec(a.shape, lambda i: (0,) * a.ndim)
    if heads[0].ndim == 3:
        specs = [pl.BlockSpec((1, tokens, rows), lambda i, j=j: (j, 0, 0)) for j in (0, 1)]
    else:
        specs = [whole(a) for a in heads]
    return call(
        project_kernel,
        (*heads, *besides, weight),
        specs + [whole(a) for a in besides] + [HBM],
        after,
        grid=(1,),
        out_specs=pl.BlockSpec((tokens, depth), lambda i: (0, 0)),
        out_shape=like((tokens, depth), dtype),
        scratch_shapes=[
            pltpu.VMEM((rows, depth), BF16),
            pltpu.VMEM((tokens, depth), F32),
            pltpu.SemaphoreType.DMA((1,)),
        ],
        cost_estimate=cost(2 * tokens * rows * depth, 4 * (tokens + rows) * depth),
        name="project",
    )


def flip(x, axis, bit):
    return lax.ppermute(x, axis, [(i, i ^ bit) for i in range(lax.axis_size(axis))])


def line(x, *pairs):
    return lax.ppermute(x, "col", pairs)


def local_grid(queries, key_vectors, value_vectors, cotangent, out_weight):
    tok_rows, features = queries.shape
    width = features // 2
    factor = float(tok_rows * lax.axis_size("row") * lax.axis_size("rep")) ** (-0.5)
    rows = out_weight.shape[0]

    def parts(h, beside, after):
        return head_parts(cotangent, cot_far, out_weight, *beside, h, after)

    own, done = attention(queries, key_vectors, value_vectors, 0, features)
    near, mid = flip(own, "col", 1), line(own, (1, 2), (2, 1))

    (half0, half1), _ = fetch_halves(out_weight, [])
    mine0, mine1 = flip(half0, "row", 1), flip(half1, "row", 1)
    cot_far = flip(cotangent, "row", 2)
    two_out, two_in = line(mid, (1, 0), (2, 3)), line(near, (1, 2), (2, 1))
    mine0 = tie(mine0, near, mid)
    beside0 = mine0, flip(mine0, "rep", 1)
    (keep0, send0), done = parts(0, beside0, [])
    got0 = flip(send0, "row", 2)
    two_in, two_out = tie(two_in, got0), tie(two_out, got0)
    three = line(two_in, (1, 0), (2, 3))
    mine1 = tie(mine1, two_in, two_out)
    beside1 = mine1, flip(mine1, "rep", 1)
    (keep1, send1), done = parts(1, beside1, [])
    got1 = flip(send1, "row", 2)
    (held, away_two, away_three), done = route_heads((own, near, two_out, two_in, three, mid), [done, got0])
    got_three = flip(away_three, "row", 2)

    (p0, p1, p2, p3), done = route_parts((keep0, got0, keep1, got1), [done])
    far = line(p3, (0, 1), (3, 2))
    held_core = flip(held, "rep", 1)
    cots = [cotangent, cot_far, flip(cotangent, "rep", 1), flip(tie(cot_far, done), "rep", 1)]
    got_three = tie(got_three, done)
    second, done = plus(p2, far, [got_three])
    out, cross = line(second, (0, 1), (3, 2)), line(second, (1, 2), (2, 1))
    got_two = flip(tie(away_two, done), "row", 2)
    heads = [held, got_three, held_core, flip(got_three, "rep", 1)]
    away, done = weight_parts(1, heads, cots, BF16, [done])
    away = flip(away, "row", 1)
    near, done = plus(p1, cross, [done])
    mid, done = plus(p3, out, [done])
    near, mid = flip(near, "col", 1), line(mid, (1, 2), (2, 1))

    besides = [*beside0, *beside1]
    sent, done = project([got_two, got_three], out_weight, besides, BF16, [done])
    from_far = flip(sent, "row", 2)
    heads = [held, got_two, held_core, flip(got_two, "rep", 1)]
    total, done = weight_parts(0, heads, cots, F32, [done])
    projected, done = project([held, held], out_weight, besides, F32, [done])
    grads, done = attention_grads_sum(queries, key_vectors, value_vectors, (p0, near, mid), [done])
    projected, done = plus(projected, from_far, [done])
    (total, grad_weight), done = weight_total(total, away, factor, rows, [done])
    grad_weight, _ = weight_fill(flip(total, "rep", 1), grad_weight)
    return (projected, *grads, grad_weight)


def local_any(queries, key_vectors, value_vectors, cotangent, out_weight):
    tok_rows, features = queries.shape
    rows = out_weight.shape[0]
    r = lax.axis_index("row")
    cot = jnp.concatenate([cotangent, flip(cotangent, "row", 2)], axis=0)
    beside = flip(out_weight, "row", 1)

    head_out, _ = attention(queries, key_vectors, value_vectors, 0, features)
    whole = lax.all_gather(head_out, "col", axis=1, tiled=True)
    held = [lax.dynamic_slice_in_dim(whole, (r ^ j) * rows, rows, 1) for j in range(4)]
    sent = flip(jnp.concatenate(held[2:], axis=1), "row", 2)
    own = jnp.concatenate([held[0], sent[:, :rows]], axis=0)
    next_to = jnp.concatenate([held[1], sent[:, rows:]], axis=0)

    part, part_beside = dot(cot, out_weight, NT), dot(cot, beside, NT)
    sent = flip(
        jnp.concatenate([part[tok_rows:], part_beside[tok_rows:]], axis=1).astype(BF16), "row", 2
    ).astype(F32)
    parts = jnp.stack([part[:tok_rows], part_beside[:tok_rows], sent[:, :rows], sent[:, rows:]])
    whole = jnp.concatenate([parts[r ^ j] for j in range(4)], axis=1)
    summed = lax.psum_scatter(whole, "col", scatter_dimension=1, tiled=True)
    grads = attention_grads(queries, key_vectors, value_vectors, summed.astype(BF16))

    factor = float(tok_rows * lax.axis_size("row") * lax.axis_size("rep")) ** (-0.5)
    away = flip(dot(next_to, cot, TN).astype(BF16), "row", 1)
    total = dot(own, cot, TN) + away.astype(F32)
    total = lax.psum(total.astype(BF16), "rep").astype(F32) * factor

    away = dot(own[tok_rows:], out_weight) + dot(next_to[tok_rows:], beside)
    away = flip(away.astype(BF16), "row", 2)
    projected = dot(own[:tok_rows], out_weight) + dot(next_to[:tok_rows], beside)
    projected = projected + away.astype(F32)
    return (projected.astype(BF16), *grads, total.astype(BF16))


def solution(mesh):
    placed = (P(("rep", "row"), "col"),) * 4 + (P("row", "col"),)
    grid = mesh.shape["col"] == 4 and mesh.shape["rep"] == 2
    return jax.shard_map(
        local_grid if grid else local_any,
        mesh=mesh,
        in_specs=placed,
        out_specs=placed,
        check_vma=False,
    )
```

```python
import functools

import jax
import jax.numpy as jnp
from jax import lax
from jax.experimental import pallas as pl
from jax.experimental.pallas import tpu as pltpu
from jax.sharding import PartitionSpec as P

HSZ = 128
PATCH = 256
SCALE = HSZ ** (-0.5)
BF16, F32 = jnp.bfloat16, jnp.float32

NN = (((1,), (0,)), ((), ()))
NT = (((1,), (1,)), ((), ()))
TN = (((0,), (0,)), ((), ()))
VMEM = pl.BlockSpec(memory_space=pltpu.VMEM)
ANY = pl.BlockSpec(memory_space=pl.ANY)
HBM = pl.BlockSpec(memory_space=pltpu.HBM)
PARAMS = pltpu.CompilerParams(vmem_limit_bytes=24 * 2**20)


def dot(a, b, dims=NN):
    return lax.dot_general(a, b, dims, preferred_element_type=F32)


def cost(macs, moved, exps=0):
    return pl.CostEstimate(flops=2 * macs, bytes_accessed=moved, transcendentals=exps)


def like(shape, dtype=BF16):
    return jax.ShapeDtypeStruct(shape, dtype)


def call(kernel, arrays, in_specs, after, out_specs, out_shape, **options):
    n, many = len(arrays), isinstance(out_shape, list)
    shapes, specs = (out_shape, out_specs) if many else ([out_shape], [out_specs])
    first = n + len(after)

    def body(*refs):
        kernel(*refs[:n], *refs[first : first + len(shapes)], *refs[first + len(shapes) + 1 :])

    *outs, mark = pl.pallas_call(
        body,
        in_specs=[*in_specs, *[ANY] * len(after)],
        out_specs=[*specs, ANY],
        out_shape=[*shapes, like((8, 128), F32)],
        compiler_params=PARAMS,
        **options,
    )(*arrays, *after)
    return (outs if many else outs[0]), mark


def tie(x, *after):
    return call(
        lambda *refs: None,
        (x,),
        [ANY],
        after,
        ANY,
        like(x.shape, x.dtype),
        input_output_aliases={0: 0},
        cost_estimate=cost(0, 0),
        name="tie",
    )[0]


def position():
    z = lax.axis_index("col")
    return lax.axis_index("row") ^ z, lax.axis_index("rep"), lax.rem(z, 3) == 0


def plus_kernel(a_ref, b_ref, out_ref):
    out_ref[...] = (a_ref[...].astype(F32) + b_ref[...].astype(F32)).astype(out_ref.dtype)


def plus(a, b, after=()):
    spec = pl.BlockSpec(a.shape, lambda i: (0, 0))
    return call(
        plus_kernel,
        (a, b),
        [spec] * 2,
        after,
        grid=(1,),
        out_specs=spec,
        out_shape=like(a.shape),
        cost_estimate=cost(0, 6 * a.size),
        name="plus",
    )


def copies(pairs, sems):
    started = [pltpu.make_async_copy(a, b, sems.at[i]) for i, (a, b) in enumerate(pairs)]
    for copy in started:
        copy.start()
    return started


def softmax_t(q, k):
    scores = dot(k, q, NT)
    lifted = jnp.exp((scores - jnp.max(scores, axis=0, keepdims=True)) * SCALE)
    return lifted * (1.0 / jnp.sum(lifted, axis=0, keepdims=True))


def forward_kernel(q_ref, k_ref, v_ref, o_ref):
    for lo in range(0, q_ref.shape[1], HSZ):
        cols = slice(lo, lo + HSZ)
        prob = softmax_t(q_ref[:, cols], k_ref[:, cols]).astype(BF16)
        o_ref[:, cols] = dot(prob, v_ref[:, cols], TN).astype(BF16)


def backward_head(q, k, v, g):
    prob = softmax_t(q, k)
    grad_prob = dot(v, g, NT)
    delta = jnp.sum(prob * grad_prob, axis=0, keepdims=True)
    grad_score = (prob * (grad_prob - delta) * SCALE).astype(BF16)
    return (
        dot(grad_score, k, TN).astype(BF16),
        dot(grad_score, q).astype(BF16),
        dot(prob.astype(BF16), g).astype(BF16),
    )


def backward_kernel(q_ref, k_ref, v_ref, g_ref, *grads):
    for lo in range(0, q_ref.shape[1], HSZ):
        cols = slice(lo, lo + HSZ)
        got = backward_head(q_ref[:, cols], k_ref[:, cols], v_ref[:, cols], g_ref[:, cols])
        for ref, value in zip(grads, got):
            ref[:, cols] = value


def backward_sum_kernel(q_ref, k_ref, v_ref, *refs):
    for lo in range(0, q_ref.shape[1], HSZ):
        cols = slice(lo, lo + HSZ)
        g = sum(ref[:, cols].astype(F32) for ref in refs[:-3]).astype(BF16)
        got = backward_head(q_ref[:, cols], k_ref[:, cols], v_ref[:, cols], g)
        for ref, value in zip(refs[-3:], got):
            ref[:, cols] = value


def head_width(width):
    return (2 if width % (2 * HSZ) == 0 else 1) * HSZ


def attention(q, k, v, at, width, after=()):
    wide = head_width(width)
    spec = pl.BlockSpec((PATCH, wide), lambda i, h: (i, h + at // wide))
    tokens = q.shape[0]
    return call(
        forward_kernel,
        (q, k, v),
        [spec] * 3,
        after,
        grid=(tokens // PATCH, width // wide),
        out_specs=pl.BlockSpec((PATCH, wide), lambda i, h: (i, h)),
        out_shape=like((tokens, width)),
        cost_estimate=cost(2 * tokens * PATCH * width, 8 * tokens * width),
        name="attention",
    )


def attention_grads(q, k, v, g):
    wide = head_width(q.shape[1])
    spec = pl.BlockSpec((PATCH, wide), lambda i, h: (i, h))
    tokens, width = q.shape
    return pl.pallas_call(
        backward_kernel,
        grid=(tokens // PATCH, width // wide),
        in_specs=[spec] * 4,
        out_specs=[spec] * 3,
        out_shape=[like(q.shape)] * 3,
        cost_estimate=cost(5 * tokens * PATCH * width, 14 * tokens * width),
        name="attention_grads",
    )(q, k, v, g)


def attention_grads_sum(q, k, v, terms, after):
    tokens, width = q.shape
    wide = head_width(width)
    spec = pl.BlockSpec((PATCH, wide), lambda i, h: (i, h))
    return call(
        backward_sum_kernel,
        (q, k, v, *terms),
        [spec] * (3 + len(terms)),
        after,
        grid=(tokens // PATCH, width // wide),
        out_specs=[spec] * 3,
        out_shape=[like(q.shape)] * 3,
        cost_estimate=cost(5 * tokens * PATCH * width, 18 * tokens * width),
        name="attention_grads",
    )


def fetch_halves_kernel(weight_ref, *refs):
    outs, sems = refs[:-1], refs[-1]
    half, me = outs[0].shape[0], position()[1]
    for copy in copies(
        [
            (weight_ref.at[pl.ds(pl.multiple_of((2 * h + me) * half, half), half)], out)
            for h, out in enumerate(outs)
        ],
        sems,
    ):
        copy.wait()


def fetch_halves(weight, after):
    rows, depth = weight.shape
    return call(
        fetch_halves_kernel,
        (weight,),
        [HBM],
        after,
        out_specs=[ANY] * 2,
        out_shape=[like((rows // 4, depth))] * 2,
        scratch_shapes=[pltpu.SemaphoreType.DMA((2,))],
        cost_estimate=cost(0, 2 * rows * depth),
        name="fetch_halves",
    )


def route_heads_kernel(*refs):
    m, me, outer = position()
    sources, (keep_ref, two_ref, three_ref, core_ref, sems) = refs[:6], refs[6:]
    steps = ((0, None), (1, None), (2, True), (2, False), (3, True), (3, False))
    half = core_ref.shape[2]
    cols = pl.ds(pl.multiple_of((1 - me) * half, half), half)
    targets = [keep_ref.at[0], keep_ref.at[1], two_ref, three_ref]
    for j, target in enumerate(targets):
        for source, (step, at_ends) in zip(sources, steps):
            here = (m ^ j) == step

            @pl.when(here if at_ends is None else here & (outer == at_ends))
            def _(target=target, j=j, source=source):
                pltpu.make_async_copy(source, target, sems.at[j]).start()
                if j < 2:
                    pltpu.make_async_copy(source.at[:, cols], core_ref.at[j], sems.at[4 + j]).start()

    for j, target in enumerate(targets):
        pltpu.make_async_copy(sources[0], target, sems.at[j]).wait()
        if j < 2:
            pltpu.make_async_copy(sources[0].at[:, cols], core_ref.at[j], sems.at[4 + j]).wait()


def route_heads(sources, after):
    tokens, width = sources[0].shape
    return call(
        route_heads_kernel,
        sources,
        [ANY] * 6,
        after,
        out_specs=[ANY] * 4,
        out_shape=[like((2, tokens, width)), like((tokens, width)), like((tokens, width))]
        + [like((2, tokens, width // 2))],
        scratch_shapes=[pltpu.SemaphoreType.DMA((6,))],
        cost_estimate=cost(0, 20 * sources[0].size),
        name="route_heads",
    )


def core_half_kernel(whole_ref, half_ref, sems):
    half = half_ref.shape[1]
    cols = pl.ds(pl.multiple_of((1 - position()[1]) * half, half), half)
    for copy in copies([(whole_ref.at[:, cols], half_ref)], sems):
        copy.wait()


def core_half(whole, after=()):
    tokens, width = whole.shape
    return call(
        core_half_kernel,
        (whole,),
        [ANY],
        after,
        out_specs=ANY,
        out_shape=like((tokens, width // 2)),
        scratch_shapes=[pltpu.SemaphoreType.DMA((1,))],
        cost_estimate=cost(0, 2 * whole.size),
        name="core_half",
    )


def head_parts_kernel(at, cot_ref, far_ref, mine_ref, other_ref, w_ref, keep_ref, send_ref, w, sems):
    (load,) = copies([(w_ref.at[pl.ds(at, w.shape[0])], w)], sems)
    m, me, _ = position()
    low, half = m & 1, mine_ref.shape[0]
    sides = ((far_ref, send_ref), (cot_ref, keep_ref))
    for source, target in sides:
        for ref, i in ((mine_ref, me), (other_ref, 1 - me)):
            cols = pl.ds(pl.multiple_of(i * half, half), half)
            target[1 - low, :, cols] = dot(source[...], ref[...], NT).astype(BF16)
    load.wait()
    for source, target in sides:
        target[low] = dot(source[...], w[...], NT).astype(BF16)


def head_parts(cot, cot_far, weight, mine, other, h, after):
    tokens, depth = cot.shape
    rows = 2 * mine.shape[0]
    whole = lambda a: pl.BlockSpec(a.shape, lambda i: (0, 0))
    out = pl.BlockSpec((2, tokens, rows), lambda i: (0, 0, 0))
    return call(
        functools.partial(head_parts_kernel, h * rows),
        (cot, cot_far, mine, other, weight),
        [whole(cot)] * 2 + [whole(mine)] * 2 + [HBM],
        after,
        grid=(1,),
        out_specs=[out] * 2,
        out_shape=[like((2, tokens, rows))] * 2,
        scratch_shapes=[pltpu.VMEM((rows, depth), BF16), pltpu.SemaphoreType.DMA((1,))],
        cost_estimate=cost(4 * tokens * depth * rows, 4 * (tokens + rows) * depth + 8 * tokens * rows),
        name="head_parts",
    )


def route_parts_kernel(*refs):
    parts, targets, sems = refs[:4], refs[4:8], refs[8]
    m = position()[0]
    width = parts[0].shape[2]
    views = [target.at[:, pl.ds(h * width, width)] for target in targets for h in (0, 1)]
    for i, view in enumerate(views):
        step, h = i // 2, i % 2
        for high, source in ((step >> 1, parts[2 * h]), (1 - (step >> 1), parts[2 * h + 1])):

            @pl.when(m >> 1 == high)
            def _(view=view, i=i, source=source.at[step & 1]):
                pltpu.make_async_copy(source, view, sems.at[i]).start()

    for i, view in enumerate(views):
        pltpu.make_async_copy(parts[0].at[0], view, sems.at[i]).wait()


def route_parts(parts, after):
    _, tokens, width = parts[0].shape
    return call(
        route_parts_kernel,
        parts,
        [ANY] * 4,
        after,
        out_specs=[ANY] * 4,
        out_shape=[like((tokens, 2 * width))] * 4,
        scratch_shapes=[pltpu.SemaphoreType.DMA((8,))],
        cost_estimate=cost(0, 16 * parts[0].size),
        name="route_parts",
    )


def weight_parts_kernel(held_ref, got_ref, held_core_ref, got_core_ref, *refs):
    cots, out_ref = refs[:4], refs[4]
    half = out_ref.shape[0]
    cols = pl.ds(pl.multiple_of(position()[1] * half, half), half)
    left = [held_ref[0, :, cols], got_ref[:, cols], held_core_ref[0], got_core_ref[...]]
    right = jnp.concatenate([ref[...] for ref in cots], axis=0)
    out_ref[...] = dot(jnp.concatenate(left, axis=0), right, TN).astype(out_ref.dtype)


def weight_parts(j, heads, cots, dtype, after):
    tokens, rows = heads[1].shape
    depth = cots[0].shape[1]
    wide = depth // 3 if depth % 384 == 0 else depth
    pair = lambda width: pl.BlockSpec((1, tokens, width), lambda i: (j, 0, 0))
    whole = lambda width: pl.BlockSpec((tokens, width), lambda i: (0, 0))
    return call(
        weight_parts_kernel,
        (*heads, *cots),
        [pair(rows), whole(rows), pair(rows // 2), whole(rows // 2)]
        + [pl.BlockSpec((tokens, wide), lambda i: (0, i))] * 4,
        after,
        grid=(depth // wide,),
        out_specs=pl.BlockSpec((rows // 2, wide), lambda i: (0, i)),
        out_shape=like((rows // 2, depth), dtype),
        cost_estimate=cost(2 * tokens * rows * depth, 8 * tokens * (rows + depth) + rows * depth),
        name="weight_parts",
    )


def weight_total(own, away, factor, rows, after):
    half, depth = own.shape
    cut = half // 2

    def kernel(own_ref, away_ref, total_ref, out_ref, own, away, total, sems):
        at = position()[1] * half
        loads, stores = [], []
        for i in (0, 1):
            part = pl.ds(i * cut, cut)
            loads.append(
                copies([(own_ref.at[part], own.at[part]), (away_ref.at[part], away.at[part])], sems.at[i])
            )
        for i, load in enumerate(loads):
            part = pl.ds(i * cut, cut)
            for copy in load:
                copy.wait()
            total[part] = ((own[part] + away[part].astype(F32)) * factor).astype(BF16)
            place = out_ref.at[pl.ds(pl.multiple_of(at + i * cut, cut), cut)]
            stores += copies([(total.at[part], total_ref.at[part]), (total.at[part], place)], sems.at[2 + i])
        for copy in stores:
            copy.wait()

    return call(
        kernel,
        (own, away),
        [ANY] * 2,
        after,
        out_specs=[ANY] * 2,
        out_shape=[like((half, depth)), like((rows, depth))],
        scratch_shapes=[
            pltpu.VMEM((half, depth), F32),
            pltpu.VMEM((half, depth), BF16),
            pltpu.VMEM((half, depth), BF16),
            pltpu.SemaphoreType.DMA((4, 2)),
        ],
        cost_estimate=cost(0, 10 * half * depth),
        name="weight_total",
    )


def weight_fill_kernel(other_ref, held_ref, out_ref, sems):
    half = other_ref.shape[0]
    at = pl.multiple_of((1 - position()[1]) * half, half)
    for copy in copies([(other_ref, out_ref.at[pl.ds(at, half)])], sems):
        copy.wait()


def weight_fill(other, held, after=()):
    return call(
        weight_fill_kernel,
        (other, held),
        [ANY] * 2,
        after,
        out_specs=ANY,
        out_shape=like(held.shape),
        scratch_shapes=[pltpu.SemaphoreType.DMA((1,))],
        input_output_aliases={1: 0},
        cost_estimate=cost(0, 4 * other.size),
        name="weight_fill",
    )


def project_kernel(own_ref, beside_ref, *refs):
    besides, weight_ref, out_ref, weight, total, sems = refs[:4], *refs[4:]
    (load,) = copies([(weight_ref, weight)], sems)
    me = position()[1]
    half = besides[0].shape[0]
    for i, ref in enumerate(besides):
        at = i // 2 * 2 + (1 - me if i % 2 else me)
        cols = pl.ds(pl.multiple_of(at * half, half), half)
        block = beside_ref[0, :, cols] if len(beside_ref.shape) == 3 else beside_ref[:, cols]
        term = dot(block, ref[...])
        total[...] = term if i == 0 else total[...] + term
    load.wait()
    total[...] += dot(own_ref[0] if len(own_ref.shape) == 3 else own_ref[...], weight[...])
    out_ref[...] = total[...].astype(out_ref.dtype)


def project(heads, weight, besides, dtype, after):
    rows, depth = weight.shape
    tokens = heads[0].shape[-2]
    whole = lambda a: pl.BlockSpec(a.shape, lambda i: (0,) * a.ndim)
    if heads[0].ndim == 3:
        specs = [pl.BlockSpec((1, tokens, rows), lambda i, j=j: (j, 0, 0)) for j in (0, 1)]
    else:
        specs = [whole(a) for a in heads]
    return call(
        project_kernel,
        (*heads, *besides, weight),
        specs + [whole(a) for a in besides] + [HBM],
        after,
        grid=(1,),
        out_specs=pl.BlockSpec((tokens, depth), lambda i: (0, 0)),
        out_shape=like((tokens, depth), dtype),
        scratch_shapes=[
            pltpu.VMEM((rows, depth), BF16),
            pltpu.VMEM((tokens, depth), F32),
            pltpu.SemaphoreType.DMA((1,)),
        ],
        cost_estimate=cost(2 * tokens * rows * depth, 4 * (tokens + rows) * depth),
        name="project",
    )


def flip(x, axis, bit):
    return lax.ppermute(x, axis, [(i, i ^ bit) for i in range(lax.axis_size(axis))])


def line(x, *pairs):
    return lax.ppermute(x, "col", pairs)


def local_grid(queries, key_vectors, value_vectors, cotangent, out_weight):
    tok_rows, features = queries.shape
    width = features // 2
    factor = float(tok_rows * lax.axis_size("row") * lax.axis_size("rep")) ** (-0.5)
    rows = out_weight.shape[0]

    def parts(h, beside, after):
        return head_parts(cotangent, cot_far, out_weight, *beside, h, after)

    own, done = attention(queries, key_vectors, value_vectors, 0, features)
    near, mid = flip(own, "col", 1), line(own, (1, 2), (2, 1))

    (half0, half1), _ = fetch_halves(out_weight, [])
    mine0, mine1 = flip(half0, "row", 1), flip(half1, "row", 1)
    cot_far = flip(cotangent, "row", 2)
    two_out, two_in = line(mid, (1, 0), (2, 3)), line(near, (1, 2), (2, 1))
    cot_core = flip(cotangent, "rep", 1)
    mine0 = tie(mine0, near, mid, cot_far, cot_core)
    beside0 = mine0, flip(mine0, "rep", 1)
    (keep0, send0), done = parts(0, beside0, [])
    far_core = flip(tie(cot_far, done), "rep", 1)
    got0 = flip(send0, "row", 2)
    two_in, two_out = tie(two_in, got0), tie(two_out, got0)
    three = line(two_in, (1, 0), (2, 3))
    mine1 = tie(mine1, two_in, two_out)
    beside1 = mine1, flip(mine1, "rep", 1)
    (keep1, send1), done = parts(1, beside1, [])
    got1 = flip(send1, "row", 2)
    (held, away_two, away_three, core), done = route_heads(
        (own, near, two_out, two_in, three, mid), [done, got0, far_core]
    )
    got_three = flip(away_three, "row", 2)

    (p0, p1, p2, p3), done = route_parts((keep0, got0, keep1, got1), [done])
    far = line(p3, (0, 1), (3, 2))
    held_core = flip(core, "rep", 1)
    cots = [cotangent, cot_far, cot_core, far_core]
    got_three = tie(got_three, done)
    got_two = flip(tie(away_two, got_three), "row", 2)
    half, done = core_half(got_three)
    second, done = plus(p2, far, [done])
    out, cross = line(second, (0, 1), (3, 2)), line(second, (1, 2), (2, 1))
    away, done = weight_parts(1, [held, got_three, held_core, flip(half, "rep", 1)], cots, BF16, [done])
    away = flip(away, "row", 1)
    besides = [*beside0, *beside1]
    projected, done = project([held, held], out_weight, besides, F32, [done])
    sent, done = project([got_two, got_three], out_weight, besides, BF16, [done])
    from_far = flip(sent, "row", 2)
    near, done = plus(p1, cross, [done])
    mid, done = plus(p3, out, [done])
    near, mid = flip(near, "col", 1), line(mid, (1, 2), (2, 1))
    half, done = core_half(got_two, [done])
    total, done = weight_parts(0, [held, got_two, held_core, flip(half, "rep", 1)], cots, F32, [done])
    projected, done = plus(projected, from_far, [done])
    (total, grad_weight), done = weight_total(total, away, factor, rows, [done, near, mid])
    grads, done = attention_grads_sum(queries, key_vectors, value_vectors, (p0, near, mid), [done])
    grad_weight, _ = weight_fill(flip(total, "rep", 1), grad_weight, [done])
    return (projected, *grads, grad_weight)


def local_any(queries, key_vectors, value_vectors, cotangent, out_weight):
    tok_rows, features = queries.shape
    rows = out_weight.shape[0]
    r = lax.axis_index("row")
    cot = jnp.concatenate([cotangent, flip(cotangent, "row", 2)], axis=0)
    beside = flip(out_weight, "row", 1)

    head_out, _ = attention(queries, key_vectors, value_vectors, 0, features)
    whole = lax.all_gather(head_out, "col", axis=1, tiled=True)
    held = [lax.dynamic_slice_in_dim(whole, (r ^ j) * rows, rows, 1) for j in range(4)]
    sent = flip(jnp.concatenate(held[2:], axis=1), "row", 2)
    own = jnp.concatenate([held[0], sent[:, :rows]], axis=0)
    next_to = jnp.concatenate([held[1], sent[:, rows:]], axis=0)

    part, part_beside = dot(cot, out_weight, NT), dot(cot, beside, NT)
    sent = flip(
        jnp.concatenate([part[tok_rows:], part_beside[tok_rows:]], axis=1).astype(BF16), "row", 2
    ).astype(F32)
    parts = jnp.stack([part[:tok_rows], part_beside[:tok_rows], sent[:, :rows], sent[:, rows:]])
    whole = jnp.concatenate([parts[r ^ j] for j in range(4)], axis=1)
    summed = lax.psum_scatter(whole, "col", scatter_dimension=1, tiled=True)
    grads = attention_grads(queries, key_vectors, value_vectors, summed.astype(BF16))

    factor = float(tok_rows * lax.axis_size("row") * lax.axis_size("rep")) ** (-0.5)
    away = flip(dot(next_to, cot, TN).astype(BF16), "row", 1)
    total = dot(own, cot, TN) + away.astype(F32)
    total = lax.psum(total.astype(BF16), "rep").astype(F32) * factor

    away = dot(own[tok_rows:], out_weight) + dot(next_to[tok_rows:], beside)
    away = flip(away.astype(BF16), "row", 2)
    projected = dot(own[:tok_rows], out_weight) + dot(next_to[:tok_rows], beside)
    projected = projected + away.astype(F32)
    return (projected.astype(BF16), *grads, total.astype(BF16))


def solution(mesh):
    placed = (P(("rep", "row"), "col"),) * 4 + (P("row", "col"),)
    grid = mesh.shape["col"] == 4 and mesh.shape["rep"] == 2
    return jax.shard_map(
        local_grid if grid else local_any,
        mesh=mesh,
        in_specs=placed,
        out_specs=placed,
        check_vma=False,
    )
```

```python
import functools

import jax
import jax.numpy as jnp
from jax import lax
from jax.experimental import pallas as pl
from jax.experimental.pallas import tpu as pltpu
from jax.sharding import PartitionSpec as P

HSZ = 128
PATCH = 256
SCALE = HSZ ** (-0.5)
BF16, F32 = jnp.bfloat16, jnp.float32

NN = (((1,), (0,)), ((), ()))
NT = (((1,), (1,)), ((), ()))
TN = (((0,), (0,)), ((), ()))
VMEM = pl.BlockSpec(memory_space=pltpu.VMEM)
ANY = pl.BlockSpec(memory_space=pl.ANY)
HBM = pl.BlockSpec(memory_space=pltpu.HBM)
PARAMS = pltpu.CompilerParams(vmem_limit_bytes=24 * 2**20)


def dot(a, b, dims=NN):
    return lax.dot_general(a, b, dims, preferred_element_type=F32)


def cost(macs, moved, exps=0):
    return pl.CostEstimate(flops=2 * macs, bytes_accessed=moved, transcendentals=exps)


def like(shape, dtype=BF16):
    return jax.ShapeDtypeStruct(shape, dtype)


def call(kernel, arrays, in_specs, after, out_specs, out_shape, **options):
    n, many = len(arrays), isinstance(out_shape, list)
    shapes, specs = (out_shape, out_specs) if many else ([out_shape], [out_specs])
    first = n + len(after)

    def body(*refs):
        kernel(*refs[:n], *refs[first : first + len(shapes)], *refs[first + len(shapes) + 1 :])

    *outs, mark = pl.pallas_call(
        body,
        in_specs=[*in_specs, *[ANY] * len(after)],
        out_specs=[*specs, ANY],
        out_shape=[*shapes, like((8, 128), F32)],
        compiler_params=PARAMS,
        **options,
    )(*arrays, *after)
    return (outs if many else outs[0]), mark


def tie(x, *after):
    return call(
        lambda *refs: None,
        (x,),
        [ANY],
        after,
        ANY,
        like(x.shape, x.dtype),
        input_output_aliases={0: 0},
        cost_estimate=cost(0, 0),
        name="tie",
    )[0]


def position():
    z = lax.axis_index("col")
    return lax.axis_index("row") ^ z, lax.axis_index("rep"), lax.rem(z, 3) == 0


def plus_kernel(a_ref, b_ref, out_ref):
    out_ref[...] = (a_ref[...].astype(F32) + b_ref[...].astype(F32)).astype(out_ref.dtype)


def plus(a, b, after=()):
    spec = pl.BlockSpec(a.shape, lambda i: (0, 0))
    return call(
        plus_kernel,
        (a, b),
        [spec] * 2,
        after,
        grid=(1,),
        out_specs=spec,
        out_shape=like(a.shape),
        cost_estimate=cost(0, 6 * a.size),
        name="plus",
    )


def copies(pairs, sems):
    started = [pltpu.make_async_copy(a, b, sems.at[i]) for i, (a, b) in enumerate(pairs)]
    for copy in started:
        copy.start()
    return started


def softmax_t(q, k):
    scores = dot(k, q, NT)
    lifted = jnp.exp((scores - jnp.max(scores, axis=0, keepdims=True)) * SCALE)
    return lifted * (1.0 / jnp.sum(lifted, axis=0, keepdims=True))


def forward_kernel(q_ref, k_ref, v_ref, o_ref):
    for lo in range(0, q_ref.shape[1], HSZ):
        cols = slice(lo, lo + HSZ)
        prob = softmax_t(q_ref[:, cols], k_ref[:, cols]).astype(BF16)
        o_ref[:, cols] = dot(prob, v_ref[:, cols], TN).astype(BF16)


def backward_head(q, k, v, g):
    prob = softmax_t(q, k)
    grad_prob = dot(v, g, NT)
    delta = jnp.sum(prob * grad_prob, axis=0, keepdims=True)
    grad_score = (prob * (grad_prob - delta) * SCALE).astype(BF16)
    return (
        dot(grad_score, k, TN).astype(BF16),
        dot(grad_score, q).astype(BF16),
        dot(prob.astype(BF16), g).astype(BF16),
    )


def backward_kernel(q_ref, k_ref, v_ref, g_ref, *grads):
    for lo in range(0, q_ref.shape[1], HSZ):
        cols = slice(lo, lo + HSZ)
        got = backward_head(q_ref[:, cols], k_ref[:, cols], v_ref[:, cols], g_ref[:, cols])
        for ref, value in zip(grads, got):
            ref[:, cols] = value


def backward_sum_kernel(q_ref, k_ref, v_ref, *refs):
    for lo in range(0, q_ref.shape[1], HSZ):
        cols = slice(lo, lo + HSZ)
        g = sum(ref[:, cols].astype(F32) for ref in refs[:-3]).astype(BF16)
        got = backward_head(q_ref[:, cols], k_ref[:, cols], v_ref[:, cols], g)
        for ref, value in zip(refs[-3:], got):
            ref[:, cols] = value


def head_width(width):
    return next(n for n in (8, 4, 2, 1) if width % (n * HSZ) == 0) * HSZ


def attention(q, k, v, at, width, after=()):
    wide = head_width(width)
    spec = pl.BlockSpec((PATCH, wide), lambda i, h: (i, h + at // wide))
    tokens = q.shape[0]
    return call(
        forward_kernel,
        (q, k, v),
        [spec] * 3,
        after,
        grid=(tokens // PATCH, width // wide),
        out_specs=pl.BlockSpec((PATCH, wide), lambda i, h: (i, h)),
        out_shape=like((tokens, width)),
        cost_estimate=cost(2 * tokens * PATCH * width, 8 * tokens * width),
        name="attention",
    )


def attention_grads(q, k, v, g):
    wide = head_width(q.shape[1])
    spec = pl.BlockSpec((PATCH, wide), lambda i, h: (i, h))
    tokens, width = q.shape
    return pl.pallas_call(
        backward_kernel,
        grid=(tokens // PATCH, width // wide),
        in_specs=[spec] * 4,
        out_specs=[spec] * 3,
        out_shape=[like(q.shape)] * 3,
        cost_estimate=cost(5 * tokens * PATCH * width, 14 * tokens * width),
        name="attention_grads",
    )(q, k, v, g)


def attention_grads_sum(q, k, v, terms, after):
    tokens, width = q.shape
    wide = head_width(width)
    spec = pl.BlockSpec((PATCH, wide), lambda i, h: (i, h))
    return call(
        backward_sum_kernel,
        (q, k, v, *terms),
        [spec] * (3 + len(terms)),
        after,
        grid=(tokens // PATCH, width // wide),
        out_specs=[spec] * 3,
        out_shape=[like(q.shape)] * 3,
        cost_estimate=cost(5 * tokens * PATCH * width, 18 * tokens * width),
        name="attention_grads",
    )


def route_heads_kernel(*refs):
    m, me, outer = position()
    sources, (keep_ref, two_ref, three_ref, core_ref, sems) = refs[:6], refs[6:]
    steps = ((0, None), (1, None), (2, True), (2, False), (3, True), (3, False))
    half = core_ref.shape[2]
    cols = pl.ds(pl.multiple_of((1 - me) * half, half), half)
    targets = [keep_ref.at[0], keep_ref.at[1], two_ref, three_ref]
    for j, target in enumerate(targets):
        for source, (step, at_ends) in zip(sources, steps):
            here = (m ^ j) == step

            @pl.when(here if at_ends is None else here & (outer == at_ends))
            def _(target=target, j=j, source=source):
                pltpu.make_async_copy(source, target, sems.at[j]).start()
                if j < 2:
                    pltpu.make_async_copy(source.at[:, cols], core_ref.at[j], sems.at[4 + j]).start()

    for j, target in enumerate(targets):
        pltpu.make_async_copy(sources[0], target, sems.at[j]).wait()
        if j < 2:
            pltpu.make_async_copy(sources[0].at[:, cols], core_ref.at[j], sems.at[4 + j]).wait()


def route_heads(sources, after):
    tokens, width = sources[0].shape
    return call(
        route_heads_kernel,
        sources,
        [ANY] * 6,
        after,
        out_specs=[ANY] * 4,
        out_shape=[like((2, tokens, width)), like((tokens, width)), like((tokens, width))]
        + [like((2, tokens, width // 2))],
        scratch_shapes=[pltpu.SemaphoreType.DMA((6,))],
        cost_estimate=cost(0, 20 * sources[0].size),
        name="route_heads",
    )


def core_half_kernel(whole_ref, half_ref, sems):
    half = half_ref.shape[1]
    cols = pl.ds(pl.multiple_of((1 - position()[1]) * half, half), half)
    for copy in copies([(whole_ref.at[:, cols], half_ref)], sems):
        copy.wait()


def core_half(whole, after=()):
    tokens, width = whole.shape
    return call(
        core_half_kernel,
        (whole,),
        [ANY],
        after,
        out_specs=ANY,
        out_shape=like((tokens, width // 2)),
        scratch_shapes=[pltpu.SemaphoreType.DMA((1,))],
        cost_estimate=cost(0, 2 * whole.size),
        name="core_half",
    )


def head_parts_kernel(n_other, cot_ref, far_ref, mine_ref, *refs):
    others, refs = refs[:n_other], refs[n_other:]
    half, me = mine_ref.shape[0], position()[1]
    whole = len(refs) > 2
    keep_ref, send_ref = refs[1:3] if whole else refs
    if whole:
        w, sems = refs[3:]
        (load,) = copies([(refs[0], w)], sems)
    rows = keep_ref.shape[1] - 2 * half
    sides = ((far_ref, send_ref), (cot_ref, keep_ref))
    pieces = [(mine_ref, rows + me * half)]
    for i, ref in enumerate(others):
        pieces.append((ref, rows + (1 - me) * half + i * ref.shape[0]))
    for source, target in sides:
        for ref, at in pieces:
            cols = pl.ds(pl.multiple_of(at, HSZ), ref.shape[0])
            target[:, cols] = dot(source[...], ref[...], NT).astype(BF16)
    if whole:
        load.wait()
        for source, target in sides:
            target[:, :rows] = dot(source[...], w[...], NT).astype(BF16)


def head_parts(cot, cot_far, mine, others, weight, after):
    tokens, depth = cot.shape
    width = 2 * mine.shape[0] + sum(a.shape[0] for a in weight)
    whole = lambda a: pl.BlockSpec(a.shape, lambda i: (0, 0))
    out = pl.BlockSpec((tokens, width), lambda i: (0, 0))
    return call(
        functools.partial(head_parts_kernel, len(others)),
        (cot, cot_far, mine, *others, *weight),
        [whole(a) for a in (cot, cot_far, mine, *others)] + [HBM] * len(weight),
        after,
        grid=(1,),
        out_specs=[out] * 2,
        out_shape=[like((tokens, width))] * 2,
        scratch_shapes=[b for a in weight for b in (pltpu.VMEM(a.shape, BF16), pltpu.SemaphoreType.DMA((1,)))],
        cost_estimate=cost(2 * tokens * depth * width, 2 * (2 * tokens + width) * depth + 4 * tokens * width),
        name="head_parts",
    )


def split_kernel(whole_ref, *refs):
    outs, sems = refs[:-1], refs[-1]
    rows = outs[0].shape[0]
    for copy in copies([(whole_ref.at[pl.ds(i * rows, rows)], out) for i, out in enumerate(outs)], sems):
        copy.wait()


def split(whole, after):
    rows, depth = whole.shape
    return call(
        split_kernel,
        (whole,),
        [ANY],
        after,
        out_specs=[ANY] * 2,
        out_shape=[like((rows // 2, depth))] * 2,
        scratch_shapes=[pltpu.SemaphoreType.DMA((2,))],
        cost_estimate=cost(0, 4 * whole.size),
        name="split",
    )[0]


def route_parts_kernel(*refs):
    (keep0, got0, keep1, got1), targets, sems = refs[:4], refs[4:8], refs[8]
    m, width = position()[0], targets[0].shape[1]
    first = keep0.shape[1] - width
    moves = []
    for j in range(4):
        big, small = (keep0, keep1) if j < 2 else (got0, got1)
        if j % 2 == 0:
            moves.append((j, big.at[:, pl.ds(0, width)], pl.ds(0, width)))
        else:
            moves.append((j, big.at[:, pl.ds(width, first)], pl.ds(0, first)))
            moves.append((j, small, pl.ds(first, width - first)))
    for i, (j, view, place) in enumerate(moves):
        for step, target in enumerate(targets):

            @pl.when((m ^ j) == step)
            def _(view=view, target=target.at[:, place], i=i):
                pltpu.make_async_copy(view, target, sems.at[i]).start()

    for i, (_, view, place) in enumerate(moves):
        pltpu.make_async_copy(view, targets[0].at[:, place], sems.at[i]).wait()


def route_parts(parts, after):
    tokens = parts[0].shape[0]
    width = (parts[0].shape[1] + parts[2].shape[1]) // 2
    return call(
        route_parts_kernel,
        parts,
        [ANY] * 4,
        after,
        out_specs=[ANY] * 4,
        out_shape=[like((tokens, width))] * 4,
        scratch_shapes=[pltpu.SemaphoreType.DMA((6,))],
        cost_estimate=cost(0, 16 * tokens * width),
        name="route_parts",
    )


def weight_parts_kernel(held_ref, got_ref, held_core_ref, got_core_ref, *refs):
    cots, out_ref = refs[:4], refs[4]
    half = out_ref.shape[0]
    cols = pl.ds(pl.multiple_of(position()[1] * half, half), half)
    left = [held_ref[0, :, cols], got_ref[:, cols], held_core_ref[0], got_core_ref[...]]
    right = jnp.concatenate([ref[...] for ref in cots], axis=0)
    out_ref[...] = dot(jnp.concatenate(left, axis=0), right, TN).astype(out_ref.dtype)


def weight_parts(j, heads, cots, dtype, after):
    tokens, rows = heads[1].shape
    depth = cots[0].shape[1]
    wide = depth // 3 if depth % 384 == 0 else depth
    pair = lambda width: pl.BlockSpec((1, tokens, width), lambda i: (j, 0, 0))
    whole = lambda width: pl.BlockSpec((tokens, width), lambda i: (0, 0))
    return call(
        weight_parts_kernel,
        (*heads, *cots),
        [pair(rows), whole(rows), pair(rows // 2), whole(rows // 2)]
        + [pl.BlockSpec((tokens, wide), lambda i: (0, i))] * 4,
        after,
        grid=(depth // wide,),
        out_specs=pl.BlockSpec((rows // 2, wide), lambda i: (0, i)),
        out_shape=like((rows // 2, depth), dtype),
        cost_estimate=cost(2 * tokens * rows * depth, 8 * tokens * (rows + depth) + rows * depth),
        name="weight_parts",
    )


def weight_total(own, away, factor, rows, after):
    half, depth = own.shape
    cut = half // 2

    def kernel(own_ref, away_ref, total_ref, out_ref, own, away, total, sems):
        at = position()[1] * half
        loads, stores = [], []
        for i in (0, 1):
            part = pl.ds(i * cut, cut)
            loads.append(
                copies([(own_ref.at[part], own.at[part]), (away_ref.at[part], away.at[part])], sems.at[i])
            )
        for i, load in enumerate(loads):
            part = pl.ds(i * cut, cut)
            for copy in load:
                copy.wait()
            total[part] = ((own[part] + away[part].astype(F32)) * factor).astype(BF16)
            place = out_ref.at[pl.ds(pl.multiple_of(at + i * cut, cut), cut)]
            stores += copies([(total.at[part], total_ref.at[part]), (total.at[part], place)], sems.at[2 + i])
        for copy in stores:
            copy.wait()

    return call(
        kernel,
        (own, away),
        [ANY] * 2,
        after,
        out_specs=[ANY] * 2,
        out_shape=[like((half, depth)), like((rows, depth))],
        scratch_shapes=[
            pltpu.VMEM((half, depth), F32),
            pltpu.VMEM((half, depth), BF16),
            pltpu.VMEM((half, depth), BF16),
            pltpu.SemaphoreType.DMA((4, 2)),
        ],
        cost_estimate=cost(0, 10 * half * depth),
        name="weight_total",
    )


def weight_fill_kernel(other_ref, held_ref, out_ref, sems):
    half = other_ref.shape[0]
    at = pl.multiple_of((1 - position()[1]) * half, half)
    for copy in copies([(other_ref, out_ref.at[pl.ds(at, half)])], sems):
        copy.wait()


def weight_fill(other, held, after=()):
    return call(
        weight_fill_kernel,
        (other, held),
        [ANY] * 2,
        after,
        out_specs=ANY,
        out_shape=like(held.shape),
        scratch_shapes=[pltpu.SemaphoreType.DMA((1,))],
        input_output_aliases={1: 0},
        cost_estimate=cost(0, 4 * other.size),
        name="weight_fill",
    )


def project_kernel(own_ref, beside_ref, *refs):
    besides, weight_ref, out_ref, weight, total, sems = refs[:-5], *refs[-5:]
    (load,) = copies([(weight_ref, weight)], sems)
    me = position()[1]
    half = besides[0].shape[0]
    starts = [me * half, (1 - me) * half, (2 + me) * half]
    for i, ref in enumerate(besides):
        at = starts[i] if i < 3 else (3 - me) * half + (i - 3) * ref.shape[0]
        cols = pl.ds(pl.multiple_of(at, HSZ), ref.shape[0])
        block = beside_ref[0, :, cols] if len(beside_ref.shape) == 3 else beside_ref[:, cols]
        term = dot(block, ref[...])
        total[...] = term if i == 0 else total[...] + term
    load.wait()
    total[...] += dot(own_ref[0] if len(own_ref.shape) == 3 else own_ref[...], weight[...])
    out_ref[...] = total[...].astype(out_ref.dtype)


def project(heads, weight, besides, dtype, after):
    rows, depth = weight.shape
    tokens = heads[0].shape[-2]
    whole = lambda a: pl.BlockSpec(a.shape, lambda i: (0,) * a.ndim)
    if heads[0].ndim == 3:
        specs = [pl.BlockSpec((1, tokens, rows), lambda i, j=j: (j, 0, 0)) for j in (0, 1)]
    else:
        specs = [whole(a) for a in heads]
    return call(
        project_kernel,
        (*heads, *besides, weight),
        specs + [whole(a) for a in besides] + [HBM],
        after,
        grid=(1,),
        out_specs=pl.BlockSpec((tokens, depth), lambda i: (0, 0)),
        out_shape=like((tokens, depth), dtype),
        scratch_shapes=[
            pltpu.VMEM((rows, depth), BF16),
            pltpu.VMEM((tokens, depth), F32),
            pltpu.SemaphoreType.DMA((1,)),
        ],
        cost_estimate=cost(2 * tokens * rows * depth, 4 * (tokens + rows) * depth),
        name="project",
    )


def flip(x, axis, bit):
    return lax.ppermute(x, axis, [(i, i ^ bit) for i in range(lax.axis_size(axis))])


def line(x, *pairs):
    return lax.ppermute(x, "col", pairs)


def local_grid(queries, key_vectors, value_vectors, cotangent, out_weight):
    tok_rows, features = queries.shape
    width = features // 2
    factor = float(tok_rows * lax.axis_size("row") * lax.axis_size("rep")) ** (-0.5)
    rows = out_weight.shape[0]

    def parts(beside, weight, after):
        return head_parts(cotangent, cot_far, beside[0], beside[1:], weight, after)

    own, done = attention(queries, key_vectors, value_vectors, 0, features)
    near, mid = flip(own, "col", 1), line(own, (1, 2), (2, 1))

    me, cut = lax.axis_index("rep"), rows // 4
    half0, half1 = [lax.dynamic_slice_in_dim(out_weight, (2 * h + me) * cut, cut, 0) for h in (0, 1)]
    mine0, mine1 = flip(half0, "row", 1), flip(half1, "row", 1)
    cot_far = flip(cotangent, "row", 2)
    two_out, two_in = line(mid, (1, 0), (2, 3)), line(near, (1, 2), (2, 1))
    cot_core = flip(cotangent, "rep", 1)
    mine0 = tie(mine0, near, mid, cot_far, cot_core)
    beside0 = mine0, flip(mine0, "rep", 1)
    (keep0, send0), done = parts(beside0, [out_weight], [])
    far_core = flip(tie(cot_far, done), "rep", 1)
    got0 = flip(send0, "row", 2)
    two_in = tie(two_in, done)
    three = line(two_in, (1, 0), (2, 3))
    mine1 = tie(mine1, two_in, two_out)
    beside1 = mine1, *(flip(a, "rep", 1) for a in split(mine1, []))
    (keep1, send1), done = parts(beside1, [], [])
    got1 = flip(send1, "row", 2)
    (held, away_two, away_three, core), done = route_heads(
        (own, near, two_out, two_in, three, mid), [done, got0, got1]
    )
    got_three = flip(away_three, "row", 2)

    (p0, p1, p2, p3), done = route_parts((keep0, got0, keep1, got1), [done])
    far = line(p3, (0, 1), (3, 2))
    held_core = flip(core, "rep", 1)
    cots = [cotangent, cot_far, cot_core, far_core]
    got_three = tie(got_three, done)
    got_two = flip(tie(away_two, got_three), "row", 2)
    half, done = core_half(got_three)
    second, done = plus(p2, far, [done])
    out, cross = line(second, (0, 1), (3, 2)), line(second, (1, 2), (2, 1))
    away, done = weight_parts(1, [held, got_three, held_core, flip(half, "rep", 1)], cots, BF16, [done])
    away = flip(away, "row", 1)
    besides = [*beside0, *beside1]
    projected, done = project([held, held], out_weight, besides, F32, [done])
    sent, done = project([got_two, got_three], out_weight, besides, BF16, [done])
    from_far = flip(sent, "row", 2)
    near, done = plus(p1, cross, [done])
    mid, done = plus(p3, out, [done])
    near, mid = flip(near, "col", 1), line(mid, (1, 2), (2, 1))
    half, done = core_half(got_two, [done])
    total, done = weight_parts(0, [held, got_two, held_core, flip(half, "rep", 1)], cots, F32, [done])
    projected, done = plus(projected, from_far, [done])
    (total, grad_weight), done = weight_total(total, away, factor, rows, [done, near, mid])
    grads, done = attention_grads_sum(queries, key_vectors, value_vectors, (p0, near, mid), [done])
    grad_weight, _ = weight_fill(flip(total, "rep", 1), grad_weight, [done])
    return (projected, *grads, grad_weight)


def local_any(queries, key_vectors, value_vectors, cotangent, out_weight):
    tok_rows, features = queries.shape
    rows = out_weight.shape[0]
    r = lax.axis_index("row")
    cot = jnp.concatenate([cotangent, flip(cotangent, "row", 2)], axis=0)
    beside = flip(out_weight, "row", 1)

    head_out, _ = attention(queries, key_vectors, value_vectors, 0, features)
    whole = lax.all_gather(head_out, "col", axis=1, tiled=True)
    held = [lax.dynamic_slice_in_dim(whole, (r ^ j) * rows, rows, 1) for j in range(4)]
    sent = flip(jnp.concatenate(held[2:], axis=1), "row", 2)
    own = jnp.concatenate([held[0], sent[:, :rows]], axis=0)
    next_to = jnp.concatenate([held[1], sent[:, rows:]], axis=0)

    part, part_beside = dot(cot, out_weight, NT), dot(cot, beside, NT)
    sent = flip(
        jnp.concatenate([part[tok_rows:], part_beside[tok_rows:]], axis=1).astype(BF16), "row", 2
    ).astype(F32)
    parts = jnp.stack([part[:tok_rows], part_beside[:tok_rows], sent[:, :rows], sent[:, rows:]])
    whole = jnp.concatenate([parts[r ^ j] for j in range(4)], axis=1)
    summed = lax.psum_scatter(whole, "col", scatter_dimension=1, tiled=True)
    grads = attention_grads(queries, key_vectors, value_vectors, summed.astype(BF16))

    factor = float(tok_rows * lax.axis_size("row") * lax.axis_size("rep")) ** (-0.5)
    away = flip(dot(next_to, cot, TN).astype(BF16), "row", 1)
    total = dot(own, cot, TN) + away.astype(F32)
    total = lax.psum(total.astype(BF16), "rep").astype(F32) * factor

    away = dot(own[tok_rows:], out_weight) + dot(next_to[tok_rows:], beside)
    away = flip(away.astype(BF16), "row", 2)
    projected = dot(own[:tok_rows], out_weight) + dot(next_to[:tok_rows], beside)
    projected = projected + away.astype(F32)
    return (projected.astype(BF16), *grads, total.astype(BF16))


def solution(mesh):
    placed = (P(("rep", "row"), "col"),) * 4 + (P("row", "col"),)
    grid = mesh.shape["col"] == 4 and mesh.shape["rep"] == 2
    return jax.shard_map(
        local_grid if grid else local_any,
        mesh=mesh,
        in_specs=placed,
        out_specs=placed,
        check_vma=False,
    )
```

```python
import functools

import jax
import jax.numpy as jnp
from jax import lax
from jax.experimental import pallas as pl
from jax.experimental.pallas import tpu as pltpu
from jax.sharding import PartitionSpec as P

HSZ = 128
PATCH = 256
SCALE = HSZ ** (-0.5)
BF16, F32 = jnp.bfloat16, jnp.float32

NN = (((1,), (0,)), ((), ()))
NT = (((1,), (1,)), ((), ()))
TN = (((0,), (0,)), ((), ()))
VMEM = pl.BlockSpec(memory_space=pltpu.VMEM)
ANY = pl.BlockSpec(memory_space=pl.ANY)
HBM = pl.BlockSpec(memory_space=pltpu.HBM)
PARAMS = pltpu.CompilerParams(vmem_limit_bytes=24 * 2**20)


def dot(a, b, dims=NN):
    return lax.dot_general(a, b, dims, preferred_element_type=F32)


def cost(macs, moved, exps=0):
    return pl.CostEstimate(flops=2 * macs, bytes_accessed=moved, transcendentals=exps)


def like(shape, dtype=BF16):
    return jax.ShapeDtypeStruct(shape, dtype)


def call(kernel, arrays, in_specs, after, out_specs, out_shape, **options):
    n, many = len(arrays), isinstance(out_shape, list)
    shapes, specs = (out_shape, out_specs) if many else ([out_shape], [out_specs])
    first = n + len(after)

    def body(*refs):
        kernel(*refs[:n], *refs[first : first + len(shapes)], *refs[first + len(shapes) + 1 :])

    *outs, mark = pl.pallas_call(
        body,
        in_specs=[*in_specs, *[ANY] * len(after)],
        out_specs=[*specs, ANY],
        out_shape=[*shapes, like((8, 128), F32)],
        compiler_params=PARAMS,
        **options,
    )(*arrays, *after)
    return (outs if many else outs[0]), mark


def tie(x, *after):
    return call(
        lambda *refs: None,
        (x,),
        [ANY],
        after,
        ANY,
        like(x.shape, x.dtype),
        input_output_aliases={0: 0},
        cost_estimate=cost(0, 0),
        name="tie",
    )[0]


def position():
    z = lax.axis_index("col")
    return lax.axis_index("row") ^ z, lax.axis_index("rep"), lax.rem(z, 3) == 0


def plus_kernel(a_ref, b_ref, out_ref):
    out_ref[...] = (a_ref[...].astype(F32) + b_ref[...].astype(F32)).astype(out_ref.dtype)


def plus(a, b, after=()):
    spec = pl.BlockSpec(a.shape, lambda i: (0, 0))
    return call(
        plus_kernel,
        (a, b),
        [spec] * 2,
        after,
        grid=(1,),
        out_specs=spec,
        out_shape=like(a.shape),
        cost_estimate=cost(0, 6 * a.size),
        name="plus",
    )


def copies(pairs, sems):
    started = [pltpu.make_async_copy(a, b, sems.at[i]) for i, (a, b) in enumerate(pairs)]
    for copy in started:
        copy.start()
    return started


def softmax_t(q, k):
    scores = dot(k, q, NT)
    lifted = jnp.exp((scores - jnp.max(scores, axis=0, keepdims=True)) * SCALE)
    return lifted * (1.0 / jnp.sum(lifted, axis=0, keepdims=True))


def forward_kernel(q_ref, k_ref, v_ref, o_ref):
    for lo in range(0, q_ref.shape[1], HSZ):
        cols = slice(lo, lo + HSZ)
        prob = softmax_t(q_ref[:, cols], k_ref[:, cols]).astype(BF16)
        o_ref[:, cols] = dot(prob, v_ref[:, cols], TN).astype(BF16)


def backward_head(q, k, v, g, prob):
    grad_prob = dot(v, g, NT)
    delta = jnp.sum(prob * grad_prob, axis=0, keepdims=True)
    grad_score = (prob * (grad_prob - delta) * SCALE).astype(BF16)
    return (
        dot(grad_score, k, TN).astype(BF16),
        dot(grad_score, q).astype(BF16),
        dot(prob.astype(BF16), g).astype(BF16),
    )


def backward_kernel(q_ref, k_ref, v_ref, g_ref, *grads):
    for lo in range(0, q_ref.shape[1], HSZ):
        cols = slice(lo, lo + HSZ)
        q, k = q_ref[:, cols], k_ref[:, cols]
        got = backward_head(q, k, v_ref[:, cols], g_ref[:, cols], softmax_t(q, k))
        for ref, value in zip(grads, got):
            ref[:, cols] = value


def backward_sum_kernel(q_ref, k_ref, v_ref, prob_ref, *refs):
    for lo in range(0, q_ref.shape[1], HSZ):
        cols = slice(lo, lo + HSZ)
        g = sum(ref[:, cols].astype(F32) for ref in refs[:-3]).astype(BF16)
        got = backward_head(q_ref[:, cols], k_ref[:, cols], v_ref[:, cols], g, prob_ref[lo // HSZ])
        for ref, value in zip(refs[-3:], got):
            ref[:, cols] = value


def head_width(width):
    return next(n for n in (8, 4, 2, 1) if width % (n * HSZ) == 0) * HSZ


def attention(q, k, v, at, width, after=()):
    wide = head_width(width)
    spec = pl.BlockSpec((PATCH, wide), lambda i, h: (i, h + at // wide))
    tokens = q.shape[0]
    return call(
        forward_kernel,
        (q, k, v),
        [spec] * 3,
        after,
        grid=(tokens // PATCH, width // wide),
        out_specs=pl.BlockSpec((PATCH, wide), lambda i, h: (i, h)),
        out_shape=like((tokens, width)),
        cost_estimate=cost(2 * tokens * PATCH * width, 8 * tokens * width),
        name="attention",
    )


def attention_grads(q, k, v, g):
    wide = head_width(q.shape[1])
    spec = pl.BlockSpec((PATCH, wide), lambda i, h: (i, h))
    tokens, width = q.shape
    return pl.pallas_call(
        backward_kernel,
        grid=(tokens // PATCH, width // wide),
        in_specs=[spec] * 4,
        out_specs=[spec] * 3,
        out_shape=[like(q.shape)] * 3,
        cost_estimate=cost(5 * tokens * PATCH * width, 14 * tokens * width),
        name="attention_grads",
    )(q, k, v, g)


def weights_kernel(q_ref, k_ref, out_ref):
    for i in range(out_ref.shape[0]):
        cols = slice(i * HSZ, (i + 1) * HSZ)
        out_ref[i] = softmax_t(q_ref[:, cols], k_ref[:, cols])


def softmax_weights(q, k, after):
    tokens, width = q.shape
    return call(
        weights_kernel,
        (q, k),
        [VMEM] * 2,
        after,
        out_specs=VMEM,
        out_shape=like((width // HSZ, tokens, tokens), F32),
        cost_estimate=cost(tokens * tokens * width, 4 * tokens * width),
        name="softmax_weights",
    )


def attention_grads_sum(q, k, v, prob, terms, after):
    tokens, width = q.shape
    return call(
        backward_sum_kernel,
        (q, k, v, prob, *terms),
        [VMEM] * (4 + len(terms)),
        after,
        grid=(1,),
        out_specs=[pl.BlockSpec(q.shape, lambda i: (0, 0))] * 3,
        out_shape=[like(q.shape)] * 3,
        cost_estimate=cost(5 * tokens * PATCH * width, 18 * tokens * width),
        name="attention_grads",
    )


def route_heads_kernel(*refs):
    m, me, outer = position()
    sources, (keep_ref, two_ref, three_ref, core_ref, sems) = refs[:6], refs[6:]
    steps = ((0, None), (1, None), (2, True), (2, False), (3, True), (3, False))
    half = core_ref.shape[2]
    cols = pl.ds(pl.multiple_of((1 - me) * half, half), half)
    targets = [keep_ref.at[0], keep_ref.at[1], two_ref, three_ref]
    for j, target in enumerate(targets):
        for source, (step, at_ends) in zip(sources, steps):
            here = (m ^ j) == step

            @pl.when(here if at_ends is None else here & (outer == at_ends))
            def _(target=target, j=j, source=source):
                pltpu.make_async_copy(source, target, sems.at[j]).start()
                if j < 2:
                    pltpu.make_async_copy(source.at[:, cols], core_ref.at[j], sems.at[4 + j]).start()

    for j, target in enumerate(targets):
        pltpu.make_async_copy(sources[0], target, sems.at[j]).wait()
        if j < 2:
            pltpu.make_async_copy(sources[0].at[:, cols], core_ref.at[j], sems.at[4 + j]).wait()


def route_heads(sources, after):
    tokens, width = sources[0].shape
    return call(
        route_heads_kernel,
        sources,
        [ANY] * 6,
        after,
        out_specs=[ANY] * 4,
        out_shape=[like((2, tokens, width)), like((tokens, width)), like((tokens, width))]
        + [like((2, tokens, width // 2))],
        scratch_shapes=[pltpu.SemaphoreType.DMA((6,))],
        cost_estimate=cost(0, 20 * sources[0].size),
        name="route_heads",
    )


def core_half_kernel(whole_ref, half_ref, sems):
    half = half_ref.shape[1]
    cols = pl.ds(pl.multiple_of((1 - position()[1]) * half, half), half)
    for copy in copies([(whole_ref.at[:, cols], half_ref)], sems):
        copy.wait()


def core_half(whole, after=()):
    tokens, width = whole.shape
    return call(
        core_half_kernel,
        (whole,),
        [ANY],
        after,
        out_specs=ANY,
        out_shape=like((tokens, width // 2)),
        scratch_shapes=[pltpu.SemaphoreType.DMA((1,))],
        cost_estimate=cost(0, 2 * whole.size),
        name="core_half",
    )


def head_parts_kernel(n_other, cot_ref, far_ref, mine_ref, *refs):
    others, refs = refs[:n_other], refs[n_other:]
    half, me = mine_ref.shape[0], position()[1]
    whole = len(refs) > 2
    keep_ref, send_ref = refs[1:3] if whole else refs
    if whole:
        w, sems = refs[3:]
        (load,) = copies([(refs[0], w)], sems)
    rows = keep_ref.shape[1] - 2 * half
    sides = ((far_ref, send_ref), (cot_ref, keep_ref))
    pieces = [(mine_ref, rows + me * half)]
    for i, ref in enumerate(others):
        pieces.append((ref, rows + (1 - me) * half + i * ref.shape[0]))
    for source, target in sides:
        for ref, at in pieces:
            cols = pl.ds(pl.multiple_of(at, HSZ), ref.shape[0])
            target[:, cols] = dot(source[...], ref[...], NT).astype(BF16)
    if whole:
        load.wait()
        for source, target in sides:
            target[:, :rows] = dot(source[...], w[...], NT).astype(BF16)


def head_parts(cot, cot_far, mine, others, weight, after):
    tokens, depth = cot.shape
    width = 2 * mine.shape[0] + sum(a.shape[0] for a in weight)
    whole = lambda a: pl.BlockSpec(a.shape, lambda i: (0, 0))
    out = pl.BlockSpec((tokens, width), lambda i: (0, 0))
    return call(
        functools.partial(head_parts_kernel, len(others)),
        (cot, cot_far, mine, *others, *weight),
        [whole(a) for a in (cot, cot_far, mine, *others)] + [HBM] * len(weight),
        after,
        grid=(1,),
        out_specs=[out] * 2,
        out_shape=[like((tokens, width))] * 2,
        scratch_shapes=[b for a in weight for b in (pltpu.VMEM(a.shape, BF16), pltpu.SemaphoreType.DMA((1,)))],
        cost_estimate=cost(2 * tokens * depth * width, 2 * (2 * tokens + width) * depth + 4 * tokens * width),
        name="head_parts",
    )


def split_kernel(whole_ref, *refs):
    outs, sems = refs[:-1], refs[-1]
    rows = outs[0].shape[0]
    for copy in copies([(whole_ref.at[pl.ds(i * rows, rows)], out) for i, out in enumerate(outs)], sems):
        copy.wait()


def split(whole, after):
    rows, depth = whole.shape
    return call(
        split_kernel,
        (whole,),
        [ANY],
        after,
        out_specs=[ANY] * 2,
        out_shape=[like((rows // 2, depth))] * 2,
        scratch_shapes=[pltpu.SemaphoreType.DMA((2,))],
        cost_estimate=cost(0, 4 * whole.size),
        name="split",
    )[0]


def route_parts_kernel(*refs):
    (keep0, got0, keep1, got1), targets, sems = refs[:4], refs[4:8], refs[8]
    m, width = position()[0], targets[0].shape[1]
    first = keep0.shape[1] - width
    moves = []
    for j in range(4):
        big, small = (keep0, keep1) if j < 2 else (got0, got1)
        if j % 2 == 0:
            moves.append((j, big.at[:, pl.ds(0, width)], pl.ds(0, width)))
        else:
            moves.append((j, big.at[:, pl.ds(width, first)], pl.ds(0, first)))
            moves.append((j, small, pl.ds(first, width - first)))
    for i, (j, view, place) in enumerate(moves):
        for step, target in enumerate(targets):

            @pl.when((m ^ j) == step)
            def _(view=view, target=target.at[:, place], i=i):
                pltpu.make_async_copy(view, target, sems.at[i]).start()

    for i, (_, view, place) in enumerate(moves):
        pltpu.make_async_copy(view, targets[0].at[:, place], sems.at[i]).wait()


def route_parts(parts, after):
    tokens = parts[0].shape[0]
    width = (parts[0].shape[1] + parts[2].shape[1]) // 2
    return call(
        route_parts_kernel,
        parts,
        [ANY] * 4,
        after,
        out_specs=[ANY] * 4,
        out_shape=[like((tokens, width))] * 4,
        scratch_shapes=[pltpu.SemaphoreType.DMA((6,))],
        cost_estimate=cost(0, 16 * tokens * width),
        name="route_parts",
    )


def weight_parts_kernel(held_ref, got_ref, held_core_ref, got_core_ref, *refs):
    cots, outs = refs[:4], refs[4:]
    half = held_core_ref.shape[2]
    cols = pl.ds(pl.multiple_of(position()[1] * half, half), half)
    left = [held_ref[0, :, cols], got_ref[:, cols], held_core_ref[0], got_core_ref[...]]
    right = jnp.concatenate([ref[...] for ref in cots], axis=0)
    total = dot(jnp.concatenate(left, axis=0), right, TN)
    at = 0
    for ref in outs:
        ref[...] = total[at : at + ref.shape[0]].astype(ref.dtype)
        at += ref.shape[0]


def weight_parts(j, heads, cots, dtype, parts, after):
    tokens, rows = heads[1].shape
    depth = cots[0].shape[1]
    wide = depth // 3 if depth % 384 == 0 else depth
    pair = lambda width: pl.BlockSpec((1, tokens, width), lambda i: (j, 0, 0))
    whole = lambda width: pl.BlockSpec((tokens, width), lambda i: (0, 0))
    sizes = [n * rows // 64 for n in parts]
    return call(
        weight_parts_kernel,
        (*heads, *cots),
        [pair(rows), whole(rows), pair(rows // 2), whole(rows // 2)]
        + [pl.BlockSpec((tokens, wide), lambda i: (0, i))] * 4,
        after,
        grid=(depth // wide,),
        out_specs=[pl.BlockSpec((size, wide), lambda i: (0, i)) for size in sizes],
        out_shape=[like((size, depth), dtype) for size in sizes],
        cost_estimate=cost(2 * tokens * rows * depth, 8 * tokens * (rows + depth) + rows * depth),
        name="weight_parts",
    )


def weight_total(own, aways, factor, rows, after):
    half, depth = own.shape
    starts = [sum(a.shape[0] for a in aways[:i]) for i in range(len(aways))]

    def kernel(own_ref, *refs):
        away_refs, (total_ref, out_ref, sems) = refs[: len(aways)], refs[len(aways) :]
        base = position()[1] * half
        stores = []
        for i, (start, ref) in enumerate(zip(starts, away_refs)):
            size = ref.shape[0]
            part = pl.ds(start, size)
            total_ref[part] = ((own_ref[part] + ref[...].astype(F32)) * factor).astype(BF16)
            target = out_ref.at[pl.ds(pl.multiple_of(base + start, 16), size)]
            stores.append(pltpu.make_async_copy(total_ref.at[part], target, sems.at[i]))
            stores[-1].start()
        for copy in stores:
            copy.wait()

    return call(
        kernel,
        (own, *aways),
        [VMEM] * (1 + len(aways)),
        after,
        out_specs=[VMEM, ANY],
        out_shape=[like((half, depth)), like((rows, depth))],
        scratch_shapes=[pltpu.SemaphoreType.DMA((len(aways),))],
        cost_estimate=cost(0, 10 * half * depth),
        name="weight_total",
    )


def weight_fill_kernel(other_ref, held_ref, out_ref, sems):
    half = other_ref.shape[0]
    at = pl.multiple_of((1 - position()[1]) * half, half)
    for copy in copies([(other_ref, out_ref.at[pl.ds(at, half)])], sems):
        copy.wait()


def weight_fill(other, held, after=()):
    return call(
        weight_fill_kernel,
        (other, held),
        [ANY] * 2,
        after,
        out_specs=ANY,
        out_shape=like(held.shape),
        scratch_shapes=[pltpu.SemaphoreType.DMA((1,))],
        input_output_aliases={1: 0},
        cost_estimate=cost(0, 4 * other.size),
        name="weight_fill",
    )


def project_kernel(own_ref, beside_ref, *refs):
    besides, weight_ref, out_ref, weight, total, sems = refs[:-5], *refs[-5:]
    (load,) = copies([(weight_ref, weight)], sems)
    me = position()[1]
    half = besides[0].shape[0]
    starts = [me * half, (1 - me) * half, (2 + me) * half]
    for i, ref in enumerate(besides):
        at = starts[i] if i < 3 else (3 - me) * half + (i - 3) * ref.shape[0]
        cols = pl.ds(pl.multiple_of(at, HSZ), ref.shape[0])
        block = beside_ref[0, :, cols] if len(beside_ref.shape) == 3 else beside_ref[:, cols]
        term = dot(block, ref[...])
        total[...] = term if i == 0 else total[...] + term
    load.wait()
    total[...] += dot(own_ref[0] if len(own_ref.shape) == 3 else own_ref[...], weight[...])
    out_ref[...] = total[...].astype(out_ref.dtype)


def project(heads, weight, besides, dtype, after):
    rows, depth = weight.shape
    tokens = heads[0].shape[-2]
    whole = lambda a: pl.BlockSpec(a.shape, lambda i: (0,) * a.ndim)
    if heads[0].ndim == 3:
        specs = [pl.BlockSpec((1, tokens, rows), lambda i, j=j: (j, 0, 0)) for j in (0, 1)]
    else:
        specs = [whole(a) for a in heads]
    return call(
        project_kernel,
        (*heads, *besides, weight),
        specs + [whole(a) for a in besides] + [HBM],
        after,
        grid=(1,),
        out_specs=pl.BlockSpec((tokens, depth), lambda i: (0, 0)),
        out_shape=like((tokens, depth), dtype),
        scratch_shapes=[
            pltpu.VMEM((rows, depth), BF16),
            pltpu.VMEM((tokens, depth), F32),
            pltpu.SemaphoreType.DMA((1,)),
        ],
        cost_estimate=cost(2 * tokens * rows * depth, 4 * (tokens + rows) * depth),
        name="project",
    )


def flip(x, axis, bit):
    return lax.ppermute(x, axis, [(i, i ^ bit) for i in range(lax.axis_size(axis))])


def line(x, *pairs):
    return lax.ppermute(x, "col", pairs)


def local_grid(queries, key_vectors, value_vectors, cotangent, out_weight):
    tok_rows, features = queries.shape
    width = features // 2
    factor = float(tok_rows * lax.axis_size("row") * lax.axis_size("rep")) ** (-0.5)
    rows = out_weight.shape[0]

    def parts(beside, weight, after):
        return head_parts(cotangent, cot_far, beside[0], beside[1:], weight, after)

    own, done = attention(queries, key_vectors, value_vectors, 0, features)
    near, mid = flip(own, "col", 1), line(own, (1, 2), (2, 1))

    me, cut = lax.axis_index("rep"), rows // 4
    half0, half1 = [lax.dynamic_slice_in_dim(out_weight, (2 * h + me) * cut, cut, 0) for h in (0, 1)]
    mine0, mine1 = flip(half0, "row", 1), flip(half1, "row", 1)
    cot_far = flip(cotangent, "row", 2)
    two_out, two_in = line(mid, (1, 0), (2, 3)), line(near, (1, 2), (2, 1))
    cot_core = flip(cotangent, "rep", 1)
    mine0 = tie(mine0, near, mid, cot_far, cot_core)
    beside0 = mine0, flip(mine0, "rep", 1)
    (keep0, send0), done = parts(beside0, [out_weight], [])
    far_core = flip(tie(cot_far, done), "rep", 1)
    got0 = flip(send0, "row", 2)
    two_in = tie(two_in, done)
    three = line(two_in, (1, 0), (2, 3))
    mine1 = tie(mine1, two_in, two_out)
    beside1 = mine1, *(flip(a, "rep", 1) for a in split(mine1, []))
    (keep1, send1), done = parts(beside1, [], [])
    got1 = flip(send1, "row", 2)
    (held, away_two, away_three, core), done = route_heads(
        (own, near, two_out, two_in, three, mid), [done, got0, got1]
    )
    got_three = flip(away_three, "row", 2)

    (p0, p1, p2, p3), done = route_parts((keep0, got0, keep1, got1), [done])
    far = line(p3, (0, 1), (3, 2))
    held_core = flip(core, "rep", 1)
    cots = [cotangent, cot_far, cot_core, far_core]
    got_three = tie(got_three, done)
    got_two = flip(tie(away_two, got_three), "row", 2)
    half, done = core_half(got_three)
    away, done = weight_parts(1, [held, got_three, held_core, flip(half, "rep", 1)], cots, BF16, (25, 7), [done])
    away = [flip(a, "row", 1) for a in away]
    second, done = plus(p2, far, [done])
    out, cross = line(second, (0, 1), (3, 2)), line(second, (1, 2), (2, 1))
    besides = [*beside0, *beside1]
    projected, done = project([held, held], out_weight, besides, F32, [done])
    sent, done = project([got_two, got_three], out_weight, besides, BF16, [done])
    from_far = flip(sent, "row", 2)
    prob, done = softmax_weights(queries, key_vectors, [done])
    near, done = plus(p1, cross, [done])
    mid, done = plus(p3, out, [done])
    near, mid = flip(near, "col", 1), line(mid, (1, 2), (2, 1))
    half, done = core_half(got_two, [done])
    (total,), done = weight_parts(0, [held, got_two, held_core, flip(half, "rep", 1)], cots, F32, (32,), [done])
    projected, done = plus(projected, from_far, [done])
    (total, grad_weight), done = weight_total(total, away, factor, rows, [done, near, mid])
    grads, done = attention_grads_sum(
        queries, key_vectors, value_vectors, prob, (p0, near, mid), [done]
    )
    grad_weight, _ = weight_fill(flip(total, "rep", 1), grad_weight, [done])
    return (projected, *grads, grad_weight)


def local_any(queries, key_vectors, value_vectors, cotangent, out_weight):
    tok_rows, features = queries.shape
    rows = out_weight.shape[0]
    r = lax.axis_index("row")
    cot = jnp.concatenate([cotangent, flip(cotangent, "row", 2)], axis=0)
    beside = flip(out_weight, "row", 1)

    head_out, _ = attention(queries, key_vectors, value_vectors, 0, features)
    whole = lax.all_gather(head_out, "col", axis=1, tiled=True)
    held = [lax.dynamic_slice_in_dim(whole, (r ^ j) * rows, rows, 1) for j in range(4)]
    sent = flip(jnp.concatenate(held[2:], axis=1), "row", 2)
    own = jnp.concatenate([held[0], sent[:, :rows]], axis=0)
    next_to = jnp.concatenate([held[1], sent[:, rows:]], axis=0)

    part, part_beside = dot(cot, out_weight, NT), dot(cot, beside, NT)
    sent = flip(
        jnp.concatenate([part[tok_rows:], part_beside[tok_rows:]], axis=1).astype(BF16), "row", 2
    ).astype(F32)
    parts = jnp.stack([part[:tok_rows], part_beside[:tok_rows], sent[:, :rows], sent[:, rows:]])
    whole = jnp.concatenate([parts[r ^ j] for j in range(4)], axis=1)
    summed = lax.psum_scatter(whole, "col", scatter_dimension=1, tiled=True)
    grads = attention_grads(queries, key_vectors, value_vectors, summed.astype(BF16))

    factor = float(tok_rows * lax.axis_size("row") * lax.axis_size("rep")) ** (-0.5)
    away = flip(dot(next_to, cot, TN).astype(BF16), "row", 1)
    total = dot(own, cot, TN) + away.astype(F32)
    total = lax.psum(total.astype(BF16), "rep").astype(F32) * factor

    away = dot(own[tok_rows:], out_weight) + dot(next_to[tok_rows:], beside)
    away = flip(away.astype(BF16), "row", 2)
    projected = dot(own[:tok_rows], out_weight) + dot(next_to[:tok_rows], beside)
    projected = projected + away.astype(F32)
    return (projected.astype(BF16), *grads, total.astype(BF16))


def solution(mesh):
    placed = (P(("rep", "row"), "col"),) * 4 + (P("row", "col"),)
    grid = mesh.shape["col"] == 4 and mesh.shape["rep"] == 2
    return jax.shard_map(
        local_grid if grid else local_any,
        mesh=mesh,
        in_specs=placed,
        out_specs=placed,
        check_vma=False,
    )
```

```python
import functools

import jax
import jax.numpy as jnp
from jax import lax
from jax.experimental import pallas as pl
from jax.experimental.pallas import tpu as pltpu
from jax.sharding import PartitionSpec as P

HSZ = 128
PATCH = 256
SCALE = HSZ ** (-0.5)
BF16, F32 = jnp.bfloat16, jnp.float32

NN = (((1,), (0,)), ((), ()))
NT = (((1,), (1,)), ((), ()))
TN = (((0,), (0,)), ((), ()))
VMEM = pl.BlockSpec(memory_space=pltpu.VMEM)
ANY = pl.BlockSpec(memory_space=pl.ANY)
HBM = pl.BlockSpec(memory_space=pltpu.HBM)
PARAMS = pltpu.CompilerParams(vmem_limit_bytes=24 * 2**20)


def dot(a, b, dims=NN):
    return lax.dot_general(a, b, dims, preferred_element_type=F32)


def cost(macs, moved, exps=0):
    return pl.CostEstimate(flops=2 * macs, bytes_accessed=moved, transcendentals=exps)


def like(shape, dtype=BF16):
    return jax.ShapeDtypeStruct(shape, dtype)


def call(kernel, arrays, in_specs, after, out_specs, out_shape, **options):
    n, many = len(arrays), isinstance(out_shape, list)
    shapes, specs = (out_shape, out_specs) if many else ([out_shape], [out_specs])
    first = n + len(after)

    def body(*refs):
        kernel(*refs[:n], *refs[first : first + len(shapes)], *refs[first + len(shapes) + 1 :])

    *outs, mark = pl.pallas_call(
        body,
        in_specs=[*in_specs, *[ANY] * len(after)],
        out_specs=[*specs, ANY],
        out_shape=[*shapes, like((8, 128), F32)],
        compiler_params=PARAMS,
        **options,
    )(*arrays, *after)
    return (outs if many else outs[0]), mark


def tie(x, *after):
    return call(
        lambda *refs: None,
        (x,),
        [ANY],
        after,
        ANY,
        like(x.shape, x.dtype),
        input_output_aliases={0: 0},
        cost_estimate=cost(0, 0),
        name="tie",
    )[0]


def position():
    z = lax.axis_index("col")
    return lax.axis_index("row") ^ z, lax.axis_index("rep"), lax.rem(z, 3) == 0


def plus_kernel(a_ref, b_ref, out_ref):
    out_ref[...] = (a_ref[...].astype(F32) + b_ref[...].astype(F32)).astype(out_ref.dtype)


def plus(a, b, after=()):
    spec = pl.BlockSpec(a.shape, lambda i: (0, 0))
    return call(
        plus_kernel,
        (a, b),
        [spec] * 2,
        after,
        grid=(1,),
        out_specs=spec,
        out_shape=like(a.shape),
        cost_estimate=cost(0, 6 * a.size),
        name="plus",
    )


def copies(pairs, sems):
    started = [pltpu.make_async_copy(a, b, sems.at[i]) for i, (a, b) in enumerate(pairs)]
    for copy in started:
        copy.start()
    return started


def softmax_t(q, k):
    scores = dot(k, q, NT)
    lifted = jnp.exp((scores - jnp.max(scores, axis=0, keepdims=True)) * SCALE)
    return lifted * (1.0 / jnp.sum(lifted, axis=0, keepdims=True))


def forward_kernel(q_ref, k_ref, v_ref, o_ref):
    for lo in range(0, q_ref.shape[1], HSZ):
        cols = slice(lo, lo + HSZ)
        prob = softmax_t(q_ref[:, cols], k_ref[:, cols]).astype(BF16)
        o_ref[:, cols] = dot(prob, v_ref[:, cols], TN).astype(BF16)


def backward_head(q, k, v, g, prob):
    grad_prob = dot(v, g, NT)
    delta = jnp.sum(prob * grad_prob, axis=0, keepdims=True)
    grad_score = (prob * (grad_prob - delta) * SCALE).astype(BF16)
    return (
        dot(grad_score, k, TN).astype(BF16),
        dot(grad_score, q).astype(BF16),
        dot(prob.astype(BF16), g).astype(BF16),
    )


def backward_kernel(q_ref, k_ref, v_ref, g_ref, *grads):
    for lo in range(0, q_ref.shape[1], HSZ):
        cols = slice(lo, lo + HSZ)
        q, k = q_ref[:, cols], k_ref[:, cols]
        got = backward_head(q, k, v_ref[:, cols], g_ref[:, cols], softmax_t(q, k))
        for ref, value in zip(grads, got):
            ref[:, cols] = value


def backward_sum_kernel(q_ref, k_ref, v_ref, prob_ref, *refs):
    terms, outs, stages, sems = refs[:-7], refs[-7:-4], refs[-4:-1], refs[-1]
    stores, step = [], 2 * HSZ
    for lo in range(0, q_ref.shape[1], HSZ):
        cols = slice(lo, lo + HSZ)
        g = sum(ref[:, cols].astype(F32) for ref in terms).astype(BF16)
        got = backward_head(q_ref[:, cols], k_ref[:, cols], v_ref[:, cols], g, prob_ref[lo // HSZ])
        for ref, value in zip(stages, got):
            ref[:, cols] = value
        if (lo + HSZ) % step == 0:
            part = pl.ds(lo + HSZ - step, step)
            pairs = [(a.at[:, part], b.at[:, part]) for a, b in zip(stages, outs)]
            stores += copies(pairs, sems.at[lo // step])
    for copy in stores:
        copy.wait()


def head_width(width):
    return next(n for n in (8, 4, 2, 1) if width % (n * HSZ) == 0) * HSZ


def attention(q, k, v, at, width, after=()):
    wide = head_width(width)
    spec = pl.BlockSpec((PATCH, wide), lambda i, h: (i, h + at // wide))
    tokens = q.shape[0]
    return call(
        forward_kernel,
        (q, k, v),
        [spec] * 3,
        after,
        grid=(tokens // PATCH, width // wide),
        out_specs=pl.BlockSpec((PATCH, wide), lambda i, h: (i, h)),
        out_shape=like((tokens, width)),
        cost_estimate=cost(2 * tokens * PATCH * width, 8 * tokens * width),
        name="attention",
    )


def attention_grads(q, k, v, g):
    wide = head_width(q.shape[1])
    spec = pl.BlockSpec((PATCH, wide), lambda i, h: (i, h))
    tokens, width = q.shape
    return pl.pallas_call(
        backward_kernel,
        grid=(tokens // PATCH, width // wide),
        in_specs=[spec] * 4,
        out_specs=[spec] * 3,
        out_shape=[like(q.shape)] * 3,
        cost_estimate=cost(5 * tokens * PATCH * width, 14 * tokens * width),
        name="attention_grads",
    )(q, k, v, g)


def weights_kernel(q_ref, k_ref, out_ref):
    for i in range(out_ref.shape[0]):
        cols = slice(i * HSZ, (i + 1) * HSZ)
        out_ref[i] = softmax_t(q_ref[:, cols], k_ref[:, cols])


def softmax_weights(q, k, after):
    tokens, width = q.shape
    return call(
        weights_kernel,
        (q, k),
        [VMEM] * 2,
        after,
        out_specs=VMEM,
        out_shape=like((width // HSZ, tokens, tokens), F32),
        cost_estimate=cost(tokens * tokens * width, 4 * tokens * width),
        name="softmax_weights",
    )


def attention_grads_sum(q, k, v, prob, terms, after):
    tokens, width = q.shape
    return call(
        backward_sum_kernel,
        (q, k, v, prob, *terms),
        [VMEM] * (4 + len(terms)),
        after,
        out_specs=[ANY] * 3,
        out_shape=[like(q.shape)] * 3,
        scratch_shapes=[pltpu.VMEM(q.shape, BF16)] * 3
        + [pltpu.SemaphoreType.DMA((width // (2 * HSZ), 3))],
        cost_estimate=cost(5 * tokens * PATCH * width, 18 * tokens * width),
        name="attention_grads",
    )


def route_heads_kernel(*refs):
    m, me, outer = position()
    sources, (keep_ref, two_ref, three_ref, core_ref, sems) = refs[:6], refs[6:]
    steps = ((0, None), (1, None), (2, True), (2, False), (3, True), (3, False))
    half = core_ref.shape[2]
    cols = pl.ds(pl.multiple_of((1 - me) * half, half), half)
    targets = [keep_ref.at[0], keep_ref.at[1], two_ref, three_ref]
    for j, target in enumerate(targets):
        for source, (step, at_ends) in zip(sources, steps):
            here = (m ^ j) == step

            @pl.when(here if at_ends is None else here & (outer == at_ends))
            def _(target=target, j=j, source=source):
                pltpu.make_async_copy(source, target, sems.at[j]).start()
                if j < 2:
                    pltpu.make_async_copy(source.at[:, cols], core_ref.at[j], sems.at[4 + j]).start()

    for j, target in enumerate(targets):
        pltpu.make_async_copy(sources[0], target, sems.at[j]).wait()
        if j < 2:
            pltpu.make_async_copy(sources[0].at[:, cols], core_ref.at[j], sems.at[4 + j]).wait()


def route_heads(sources, after):
    tokens, width = sources[0].shape
    return call(
        route_heads_kernel,
        sources,
        [ANY] * 6,
        after,
        out_specs=[ANY] * 4,
        out_shape=[like((2, tokens, width)), like((tokens, width)), like((tokens, width))]
        + [like((2, tokens, width // 2))],
        scratch_shapes=[pltpu.SemaphoreType.DMA((6,))],
        cost_estimate=cost(0, 20 * sources[0].size),
        name="route_heads",
    )


def core_half_kernel(whole_ref, half_ref, sems):
    half = half_ref.shape[1]
    cols = pl.ds(pl.multiple_of((1 - position()[1]) * half, half), half)
    for copy in copies([(whole_ref.at[:, cols], half_ref)], sems):
        copy.wait()


def core_half(whole, after=()):
    tokens, width = whole.shape
    return call(
        core_half_kernel,
        (whole,),
        [ANY],
        after,
        out_specs=ANY,
        out_shape=like((tokens, width // 2)),
        scratch_shapes=[pltpu.SemaphoreType.DMA((1,))],
        cost_estimate=cost(0, 2 * whole.size),
        name="core_half",
    )


def head_parts_kernel(n_other, cot_ref, far_ref, mine_ref, *refs):
    others, refs = refs[:n_other], refs[n_other:]
    half, me = mine_ref.shape[0], position()[1]
    whole = len(refs) > 2
    keep_ref, send_ref = refs[1:3] if whole else refs
    if whole:
        w, sems = refs[3:]
        (load,) = copies([(refs[0], w)], sems)
    rows = keep_ref.shape[1] - 2 * half
    sides = ((far_ref, send_ref), (cot_ref, keep_ref))
    pieces = [(mine_ref, rows + me * half)]
    for i, ref in enumerate(others):
        pieces.append((ref, rows + (1 - me) * half + i * ref.shape[0]))
    for source, target in sides:
        for ref, at in pieces:
            cols = pl.ds(pl.multiple_of(at, HSZ), ref.shape[0])
            target[:, cols] = dot(source[...], ref[...], NT).astype(BF16)
    if whole:
        load.wait()
        for source, target in sides:
            target[:, :rows] = dot(source[...], w[...], NT).astype(BF16)


def head_parts(cot, cot_far, mine, others, weight, after):
    tokens, depth = cot.shape
    width = 2 * mine.shape[0] + sum(a.shape[0] for a in weight)
    whole = lambda a: pl.BlockSpec(a.shape, lambda i: (0, 0))
    out = pl.BlockSpec((tokens, width), lambda i: (0, 0))
    return call(
        functools.partial(head_parts_kernel, len(others)),
        (cot, cot_far, mine, *others, *weight),
        [whole(a) for a in (cot, cot_far, mine, *others)] + [HBM] * len(weight),
        after,
        grid=(1,),
        out_specs=[out] * 2,
        out_shape=[like((tokens, width))] * 2,
        scratch_shapes=[b for a in weight for b in (pltpu.VMEM(a.shape, BF16), pltpu.SemaphoreType.DMA((1,)))],
        cost_estimate=cost(2 * tokens * depth * width, 2 * (2 * tokens + width) * depth + 4 * tokens * width),
        name="head_parts",
    )


def split_kernel(whole_ref, *refs):
    outs, sems = refs[:-1], refs[-1]
    rows = outs[0].shape[0]
    for copy in copies([(whole_ref.at[pl.ds(i * rows, rows)], out) for i, out in enumerate(outs)], sems):
        copy.wait()


def split(whole, after):
    rows, depth = whole.shape
    return call(
        split_kernel,
        (whole,),
        [ANY],
        after,
        out_specs=[ANY] * 2,
        out_shape=[like((rows // 2, depth))] * 2,
        scratch_shapes=[pltpu.SemaphoreType.DMA((2,))],
        cost_estimate=cost(0, 4 * whole.size),
        name="split",
    )[0]


def route_parts_kernel(*refs):
    (keep0, got0, keep1, got1), targets, sems = refs[:4], refs[4:8], refs[8]
    m, width = position()[0], targets[0].shape[1]
    first = keep0.shape[1] - width
    moves = []
    for j in range(4):
        big, small = (keep0, keep1) if j < 2 else (got0, got1)
        if j % 2 == 0:
            moves.append((j, big.at[:, pl.ds(0, width)], pl.ds(0, width)))
        else:
            moves.append((j, big.at[:, pl.ds(width, first)], pl.ds(0, first)))
            moves.append((j, small, pl.ds(first, width - first)))
    for i, (j, view, place) in enumerate(moves):
        for step, target in enumerate(targets):

            @pl.when((m ^ j) == step)
            def _(view=view, target=target.at[:, place], i=i):
                pltpu.make_async_copy(view, target, sems.at[i]).start()

    for i, (_, view, place) in enumerate(moves):
        pltpu.make_async_copy(view, targets[0].at[:, place], sems.at[i]).wait()


def route_parts(parts, after):
    tokens = parts[0].shape[0]
    width = (parts[0].shape[1] + parts[2].shape[1]) // 2
    return call(
        route_parts_kernel,
        parts,
        [ANY] * 4,
        after,
        out_specs=[ANY] * 4,
        out_shape=[like((tokens, width))] * 4,
        scratch_shapes=[pltpu.SemaphoreType.DMA((6,))],
        cost_estimate=cost(0, 16 * tokens * width),
        name="route_parts",
    )


def weight_parts_kernel(held_ref, got_ref, held_core_ref, got_core_ref, *refs):
    cots, outs = refs[:4], refs[4:]
    half = held_core_ref.shape[2]
    cols = pl.ds(pl.multiple_of(position()[1] * half, half), half)
    left = [held_ref[0, :, cols], got_ref[:, cols], held_core_ref[0], got_core_ref[...]]
    right = jnp.concatenate([ref[...] for ref in cots], axis=0)
    total = dot(jnp.concatenate(left, axis=0), right, TN)
    at = 0
    for ref in outs:
        ref[...] = total[at : at + ref.shape[0]].astype(ref.dtype)
        at += ref.shape[0]


def weight_parts(j, heads, cots, dtype, parts, after):
    tokens, rows = heads[1].shape
    depth = cots[0].shape[1]
    wide = depth // 3 if depth % 384 == 0 else depth
    pair = lambda width: pl.BlockSpec((1, tokens, width), lambda i: (j, 0, 0))
    whole = lambda width: pl.BlockSpec((tokens, width), lambda i: (0, 0))
    sizes = [n * rows // 64 for n in parts]
    return call(
        weight_parts_kernel,
        (*heads, *cots),
        [pair(rows), whole(rows), pair(rows // 2), whole(rows // 2)]
        + [pl.BlockSpec((tokens, wide), lambda i: (0, i))] * 4,
        after,
        grid=(depth // wide,),
        out_specs=[pl.BlockSpec((size, wide), lambda i: (0, i)) for size in sizes],
        out_shape=[like((size, depth), dtype) for size in sizes],
        cost_estimate=cost(2 * tokens * rows * depth, 8 * tokens * (rows + depth) + rows * depth),
        name="weight_parts",
    )


def weight_total(own, aways, factor, rows, after):
    half, depth = own.shape
    starts = [sum(a.shape[0] for a in aways[:i]) for i in range(len(aways))]

    def kernel(own_ref, *refs):
        away_refs, (total_ref, out_ref, sems) = refs[: len(aways)], refs[len(aways) :]
        base = position()[1] * half
        stores = []
        for i, (start, ref) in enumerate(zip(starts, away_refs)):
            size = ref.shape[0]
            part = pl.ds(start, size)
            total_ref[part] = ((own_ref[part] + ref[...].astype(F32)) * factor).astype(BF16)
            target = out_ref.at[pl.ds(pl.multiple_of(base + start, 16), size)]
            stores.append(pltpu.make_async_copy(total_ref.at[part], target, sems.at[i]))
            stores[-1].start()
        for copy in stores:
            copy.wait()

    return call(
        kernel,
        (own, *aways),
        [VMEM] * (1 + len(aways)),
        after,
        out_specs=[VMEM, ANY],
        out_shape=[like((half, depth)), like((rows, depth))],
        scratch_shapes=[pltpu.SemaphoreType.DMA((len(aways),))],
        cost_estimate=cost(0, 10 * half * depth),
        name="weight_total",
    )


def weight_fill_kernel(other_ref, held_ref, out_ref, sems):
    half = other_ref.shape[0]
    at = pl.multiple_of((1 - position()[1]) * half, half)
    for copy in copies([(other_ref, out_ref.at[pl.ds(at, half)])], sems):
        copy.wait()


def weight_fill(other, held, after=()):
    return call(
        weight_fill_kernel,
        (other, held),
        [ANY] * 2,
        after,
        out_specs=ANY,
        out_shape=like(held.shape),
        scratch_shapes=[pltpu.SemaphoreType.DMA((1,))],
        input_output_aliases={1: 0},
        cost_estimate=cost(0, 4 * other.size),
        name="weight_fill",
    )


def project_kernel(own_ref, beside_ref, *refs):
    besides, weight_ref, out_ref, weight, total, sems = refs[:-5], *refs[-5:]
    (load,) = copies([(weight_ref, weight)], sems)
    me = position()[1]
    half = besides[0].shape[0]
    starts = [me * half, (1 - me) * half, (2 + me) * half]
    for i, ref in enumerate(besides):
        at = starts[i] if i < 3 else (3 - me) * half + (i - 3) * ref.shape[0]
        cols = pl.ds(pl.multiple_of(at, HSZ), ref.shape[0])
        block = beside_ref[0, :, cols] if len(beside_ref.shape) == 3 else beside_ref[:, cols]
        term = dot(block, ref[...])
        total[...] = term if i == 0 else total[...] + term
    load.wait()
    total[...] += dot(own_ref[0] if len(own_ref.shape) == 3 else own_ref[...], weight[...])
    out_ref[...] = total[...].astype(out_ref.dtype)


def project(heads, weight, besides, dtype, after):
    rows, depth = weight.shape
    tokens = heads[0].shape[-2]
    whole = lambda a: pl.BlockSpec(a.shape, lambda i: (0,) * a.ndim)
    if heads[0].ndim == 3:
        specs = [pl.BlockSpec((1, tokens, rows), lambda i, j=j: (j, 0, 0)) for j in (0, 1)]
    else:
        specs = [whole(a) for a in heads]
    return call(
        project_kernel,
        (*heads, *besides, weight),
        specs + [whole(a) for a in besides] + [HBM],
        after,
        grid=(1,),
        out_specs=pl.BlockSpec((tokens, depth), lambda i: (0, 0)),
        out_shape=like((tokens, depth), dtype),
        scratch_shapes=[
            pltpu.VMEM((rows, depth), BF16),
            pltpu.VMEM((tokens, depth), F32),
            pltpu.SemaphoreType.DMA((1,)),
        ],
        cost_estimate=cost(2 * tokens * rows * depth, 4 * (tokens + rows) * depth),
        name="project",
    )


def flip(x, axis, bit):
    return lax.ppermute(x, axis, [(i, i ^ bit) for i in range(lax.axis_size(axis))])


def line(x, *pairs):
    return lax.ppermute(x, "col", pairs)


def local_grid(queries, key_vectors, value_vectors, cotangent, out_weight):
    tok_rows, features = queries.shape
    width = features // 2
    factor = float(tok_rows * lax.axis_size("row") * lax.axis_size("rep")) ** (-0.5)
    rows = out_weight.shape[0]

    def parts(beside, weight, after):
        return head_parts(cotangent, cot_far, beside[0], beside[1:], weight, after)

    own, done = attention(queries, key_vectors, value_vectors, 0, features)
    near, mid = flip(own, "col", 1), line(own, (1, 2), (2, 1))

    me, cut = lax.axis_index("rep"), rows // 4
    half0, half1 = [lax.dynamic_slice_in_dim(out_weight, (2 * h + me) * cut, cut, 0) for h in (0, 1)]
    mine0, mine1 = flip(half0, "row", 1), flip(half1, "row", 1)
    cot_far = flip(cotangent, "row", 2)
    two_out, two_in = line(mid, (1, 0), (2, 3)), line(near, (1, 2), (2, 1))
    cot_core = flip(cotangent, "rep", 1)
    mine0 = tie(mine0, near, mid, cot_far, cot_core)
    beside0 = mine0, flip(mine0, "rep", 1)
    (keep0, send0), done = parts(beside0, [out_weight], [])
    far_core = flip(tie(cot_far, done), "rep", 1)
    got0 = flip(send0, "row", 2)
    two_in = tie(two_in, done)
    three = line(two_in, (1, 0), (2, 3))
    mine1 = tie(mine1, two_in, two_out)
    beside1 = mine1, *(flip(a, "rep", 1) for a in split(mine1, []))
    (keep1, send1), done = parts(beside1, [], [])
    got1 = flip(send1, "row", 2)
    (held, away_two, away_three, core), done = route_heads(
        (own, near, two_out, two_in, three, mid), [done, got0, got1]
    )
    got_three = flip(away_three, "row", 2)

    (p0, p1, p2, p3), done = route_parts((keep0, got0, keep1, got1), [done])
    far = line(p3, (0, 1), (3, 2))
    held_core = flip(core, "rep", 1)
    cots = [cotangent, cot_far, cot_core, far_core]
    got_three = tie(got_three, done)
    got_two = flip(tie(away_two, got_three), "row", 2)
    half, done = core_half(got_three)
    away, done = weight_parts(1, [held, got_three, held_core, flip(half, "rep", 1)], cots, BF16, (25, 7), [done])
    away = [flip(a, "row", 1) for a in away]
    second, done = plus(p2, far, [done])
    out, cross = line(second, (0, 1), (3, 2)), line(second, (1, 2), (2, 1))
    besides = [*beside0, *beside1]
    projected, done = project([held, held], out_weight, besides, F32, [done])
    sent, done = project([got_two, got_three], out_weight, besides, BF16, [done])
    from_far = flip(sent, "row", 2)
    prob, done = softmax_weights(queries, key_vectors, [done])
    near, done = plus(p1, cross, [done])
    mid, done = plus(p3, out, [done])
    near, mid = flip(near, "col", 1), line(mid, (1, 2), (2, 1))
    half, done = core_half(got_two, [done])
    (total,), done = weight_parts(0, [held, got_two, held_core, flip(half, "rep", 1)], cots, F32, (32,), [done])
    projected, done = plus(projected, from_far, [done])
    (total, grad_weight), done = weight_total(total, away, factor, rows, [done, near, mid])
    grads, done = attention_grads_sum(
        queries, key_vectors, value_vectors, prob, (p0, near, mid), [done]
    )
    grad_weight, _ = weight_fill(flip(total, "rep", 1), grad_weight, [done])
    return (projected, *grads, grad_weight)


def local_any(queries, key_vectors, value_vectors, cotangent, out_weight):
    tok_rows, features = queries.shape
    rows = out_weight.shape[0]
    r = lax.axis_index("row")
    cot = jnp.concatenate([cotangent, flip(cotangent, "row", 2)], axis=0)
    beside = flip(out_weight, "row", 1)

    head_out, _ = attention(queries, key_vectors, value_vectors, 0, features)
    whole = lax.all_gather(head_out, "col", axis=1, tiled=True)
    held = [lax.dynamic_slice_in_dim(whole, (r ^ j) * rows, rows, 1) for j in range(4)]
    sent = flip(jnp.concatenate(held[2:], axis=1), "row", 2)
    own = jnp.concatenate([held[0], sent[:, :rows]], axis=0)
    next_to = jnp.concatenate([held[1], sent[:, rows:]], axis=0)

    part, part_beside = dot(cot, out_weight, NT), dot(cot, beside, NT)
    sent = flip(
        jnp.concatenate([part[tok_rows:], part_beside[tok_rows:]], axis=1).astype(BF16), "row", 2
    ).astype(F32)
    parts = jnp.stack([part[:tok_rows], part_beside[:tok_rows], sent[:, :rows], sent[:, rows:]])
    whole = jnp.concatenate([parts[r ^ j] for j in range(4)], axis=1)
    summed = lax.psum_scatter(whole, "col", scatter_dimension=1, tiled=True)
    grads = attention_grads(queries, key_vectors, value_vectors, summed.astype(BF16))

    factor = float(tok_rows * lax.axis_size("row") * lax.axis_size("rep")) ** (-0.5)
    away = flip(dot(next_to, cot, TN).astype(BF16), "row", 1)
    total = dot(own, cot, TN) + away.astype(F32)
    total = lax.psum(total.astype(BF16), "rep").astype(F32) * factor

    away = dot(own[tok_rows:], out_weight) + dot(next_to[tok_rows:], beside)
    away = flip(away.astype(BF16), "row", 2)
    projected = dot(own[:tok_rows], out_weight) + dot(next_to[:tok_rows], beside)
    projected = projected + away.astype(F32)
    return (projected.astype(BF16), *grads, total.astype(BF16))


def solution(mesh):
    placed = (P(("rep", "row"), "col"),) * 4 + (P("row", "col"),)
    grid = mesh.shape["col"] == 4 and mesh.shape["rep"] == 2
    return jax.shard_map(
        local_grid if grid else local_any,
        mesh=mesh,
        in_specs=placed,
        out_specs=placed,
        check_vma=False,
    )
```
